32 devices in a mesh: groups: 2 (over x), tile: 4 (over y, core), sect: 4 (over z).
Axes of the slice: x: 2, y: 2, z: 4, core: 2. Of those that a mesh axis runs over, the one named last changes fastest.
Arguments:
- source_probes: float32 [2, 32, 8192], P(None, 'groups', ('tile', 'sect')), parts along dimension 1, may hold values from -6 to 6
- near_blocks: bfloat16 [4, 9, 512, 8192], P('groups', None, None, ('tile', 'sect')), parts along dimension 0, may hold values from -0.0625 to 0.0625
- bloch_angle: float32 [4], P('groups'), parts along dimension 0, may hold values from -3.140625 to 3.140625
- grid_row: int32 [8192], P(('tile', 'sect')), may hold values from 0 to 511, as said below
- grid_col: int32 [8192], P(('tile', 'sect')), may hold values from 0 to 511, as said below
- stencil: bfloat16 [4, 4, 8192], P(None, None, ('tile', 'sect')), may hold values from 0.19921875 to 1
- recip_kernel: float32 [1024, 512], P('groups', ('tile', 'sect')), parts along dimension 0, may hold values from 0.1 to 2
Outputs:
- first_image: float32 [2, 32, 8192], P(None, 'groups', ('tile', 'sect')), parts along dimension 1
- second_image: float32 [2, 32, 8192], P(None, 'groups', ('tile', 'sect')), parts along dimension 1
The draws below stay inside these ranges and needn't reach their ends.
There are 2 independent parts, one for each index of `groups`. The reference program is written for one: setup_inputs(seed, part) draws one part's arguments, and reference() takes and returns one part's arrays. A program takes and returns all parts, laid end to end along the dimension named above; an argument that names none is the same for every part. Nothing has to cross between parts.
Inputs may be any that keep to these rules, and one draw needn't show every extreme that they name: `grid_row`: panel i has its first stencil row among the 32 grid rows (i // 512) * 32 to (i // 512 + 1) * 32 - 1, and every grid row is the first row of some panel. `grid_col`: every grid column is the first column of some panel.
All inputs are finite; a program needn't handle non-finite values.
Results may differ from the reference program's by a relative error of at most 0.0032.
Values may be sent and summed in bfloat16 or wider, within the bound.
No kernel may reach another device: no remote copies, remote signals or barrier semaphores. Data moves between devices by JAX's collectives and lax.ppermute only.
A program may use at most 128 MiB of HBM per device.

```python
import math
import jax
import jax.numpy as jnp
from jax import lax

PB = 512
PROBES = 16
STENCIL = 4
NG1 = 512
NG2 = 512
PANELS = 8192
ROWS_DEV = 32
N_TILE = 4
N_SECT = 4


def draw_grid_row(key, part):

    def one_block(block):
        block_key = jax.random.fold_in(key, block)
        order_key, random_key = jax.random.split(block_key)
        shuffled = jax.random.permutation(order_key, PB)
        random_rows = jax.random.randint(random_key, (PB,), 0, ROWS_DEV)
        within_rows = jnp.where(shuffled < ROWS_DEV, shuffled, random_rows)
        return block * ROWS_DEV + within_rows
    blocks = jnp.arange(PANELS // PB, dtype=jnp.int32)
    return jax.vmap(one_block)(blocks).reshape(PANELS).astype(jnp.int32)


def draw_grid_col(key, part):
    shuffled = jax.random.permutation(jax.random.fold_in(key, 7), PANELS)
    return (shuffled % NG2).astype(jnp.int32)


def block_levels(rng, dims, shards, low, high):
    factor_of, own = 1.0, jax.random.fold_in(rng, 6)
    for dim, shards_of in shards:
        heights = jnp.exp(jax.random.uniform(jax.random.fold_in(own, dim), (shards_of,), jnp.float32, low / len(shards), high / len(shards)))
        factor_of = factor_of * jnp.repeat(heights, dims[dim] // shards_of).reshape([-1 if axis == dim else 1 for axis in range(len(dims))])
    return factor_of


def scatter_about(key, dims, width, most, shards=(), held_as=jnp.bfloat16):
    drawn = jax.random.normal(key, dims, jnp.float32) * width
    if len(shards) > 0:
        drawn = block_levels(key, dims, shards, -0.22, 0.18) * drawn
    return jnp.clip(drawn, min=-most, max=most).astype(held_as)


def setup_inputs(seed: int = 0, part: int = 0) -> dict:
    key_of = jax.random.split(jax.random.key(seed), 8)
    part_splits = jax.random.split(jax.random.fold_in(key_of[7], part), 8)
    source_probes = scatter_about(part_splits[0], (2, PROBES, PANELS), 1.0, 6.0, ((2, 16),), jnp.float32)
    near_blocks = scatter_about(part_splits[1], (2, 9, PB, PANELS), (18 * PB) ** -0.5, 0.0625, ((3, 16),))
    bloch_angle = jnp.clip(jax.random.uniform(part_splits[2], (2,), jnp.float32, -3.140625, 3.140625), -3.140625, 3.140625)
    grid_row = draw_grid_row(jax.random.fold_in(key_of[7], 71), part)
    grid_col = draw_grid_col(jax.random.fold_in(key_of[7], 71), part)
    stencil = jnp.clip(0.19921875 + 0.80078125 * jax.random.uniform(key_of[5], (STENCIL, STENCIL, PANELS), jnp.float32) ** block_levels(key_of[5], (STENCIL, STENCIL, PANELS), ((2, 16),), -0.2, 0.2), 0.19921875, 1.0).astype(jnp.bfloat16)
    recip_kernel = jnp.clip(jnp.exp(math.log(2.0) - 2.9957323 * jax.random.uniform(part_splits[6], (NG1, NG2), jnp.float32) ** block_levels(part_splits[6], (NG1, NG2), ((1, 16),), -0.2, 0.2)), 0.1, 2.0)
    return dict(source_probes=source_probes, near_blocks=near_blocks, bloch_angle=bloch_angle, grid_row=grid_row, grid_col=grid_col, stencil=stencil, recip_kernel=recip_kernel)


def near_apply(rounded, near_blocks, bloch_angle):
    blocks = rounded.reshape(2, PROBES, N_TILE, N_SECT, PB)
    weights = near_blocks.reshape(2, 9, PB, N_TILE, N_SECT, PB)
    tile_ids = jnp.arange(N_TILE)
    sect_ids = jnp.arange(N_SECT)
    total_real = jnp.zeros((PROBES, N_TILE, N_SECT, PB), jnp.float32)
    total_imag = jnp.zeros((PROBES, N_TILE, N_SECT, PB), jnp.float32)
    for tile_off in (-1, 0, 1):
        for sect_off in (-1, 0, 1):
            index = (tile_off + 1) * 3 + sect_off + 1
            shifted = jnp.roll(blocks, (-tile_off, -sect_off), axis=(2, 3))
            with_real = jnp.einsum("cptsj,jtsi->cptsi", shifted, weights[0, index].astype(jnp.float32))
            with_imag = jnp.einsum("cptsj,jtsi->cptsi", shifted, weights[1, index].astype(jnp.float32))
            part_real = with_real[0] - with_imag[1]
            part_imag = with_real[1] + with_imag[0]
            if tile_off != 0 or sect_off != 0:
                angle_tile = jnp.zeros((N_TILE,), jnp.float32)
                angle_sect = jnp.zeros((N_SECT,), jnp.float32)
                if tile_off != 0:
                    border = tile_ids == (N_TILE - 1 if tile_off == 1 else 0)
                    angle_tile = jnp.where(border, bloch_angle[0] * tile_off, 0.0)
                if sect_off != 0:
                    border = sect_ids == (N_SECT - 1 if sect_off == 1 else 0)
                    angle_sect = jnp.where(border, bloch_angle[1] * sect_off, 0.0)
                phase_angle = angle_tile[:, None] + angle_sect[None, :]
                cos_part = jnp.cos(phase_angle)[None, :, :, None]
                sin_part = jnp.sin(phase_angle)[None, :, :, None]
                part_real, part_imag = part_real * cos_part - part_imag * sin_part, part_real * sin_part + part_imag * cos_part
            total_real = total_real + part_real
            total_imag = total_imag + part_imag
    return jnp.stack([total_real, total_imag]).reshape(2, PROBES, PANELS)


def recip_apply(rounded, grid_row, grid_col, stencil, recip_kernel):
    weights = stencil.astype(jnp.float32)
    offsets = jnp.arange(STENCIL, dtype=jnp.int32)
    rows = (grid_row[None, None, :] + offsets[:, None, None]) % NG1
    cols = (grid_col[None, None, :] + offsets[None, :, None]) % NG2
    cells = rows * NG2 + cols
    values = weights[None, None, :, :, :] * rounded[:, :, None, None, :]
    grid = jnp.zeros((2, PROBES, NG1 * NG2), jnp.float32).at[:, :, cells].add(values)
    complex_grid = lax.complex(grid[0], grid[1]).reshape(PROBES, NG1, NG2)
    spectrum = jnp.fft.fft2(complex_grid) * recip_kernel
    field = jnp.fft.ifft2(spectrum).reshape(PROBES, NG1 * NG2)
    planes = jnp.stack([jnp.real(field), jnp.imag(field)]).astype(jnp.float32)
    planes = lax.optimization_barrier(planes.astype(jnp.bfloat16)).astype(jnp.float32)
    return jnp.sum(weights[None, None, :, :, :] * planes[:, :, cells], axis=(2, 3))


def apply_operator(source, near_blocks, bloch_angle, grid_row, grid_col, stencil, recip_kernel):
    rounded = lax.optimization_barrier(source.astype(jnp.bfloat16)).astype(jnp.float32)
    near_part = near_apply(rounded, near_blocks, bloch_angle)
    recip_part = recip_apply(rounded, grid_row, grid_col, stencil, recip_kernel)
    return 0.5 * source + near_part + recip_part


def reference(source_probes, near_blocks, bloch_angle, grid_row, grid_col, stencil, recip_kernel):
    first_image = apply_operator(source_probes, near_blocks, bloch_angle, grid_row, grid_col, stencil, recip_kernel)
    second_image = apply_operator(first_image, near_blocks, bloch_angle, grid_row, grid_col, stencil, recip_kernel)
    return first_image, second_image
```

```python
import functools

import jax
import jax.numpy as jnp
import ml_dtypes
import numpy as np
from jax import lax
from jax.experimental import pallas as pl
from jax.experimental.pallas import tpu as pltpu
from jax.sharding import PartitionSpec as P

STENCIL = 4
RADIX = 4
F32 = jnp.float32
BF = jnp.bfloat16
AXES = ("tile", "sect")


def split_host(x):
    hi=x.astype(ml_dtypes.bfloat16); lo=(x-hi.astype(np.float64)).astype(ml_dtypes.bfloat16)
    return hi,lo

def tables(n):
    q=n//RADIX
    k=np.arange(q)
    ang=2*np.pi*((k[:,None]*k[None,:])%q)/q
    c,s=np.cos(ang),np.sin(ang)
    A=np.block([[c,-s],[s,c]]); B=np.block([[c,s],[-s,c]])
    ah,al=split_host(A); bh,bl=split_host(B)
    mats=np.stack([ah,al,bh,bl])
    r=np.arange(RADIX)
    t=2*np.pi*(r[:,None]*k[None,:])/n
    tw=np.stack([np.cos(t),np.sin(t)],1).astype(np.float32)
    return mats,tw

def dot(a,b): return jnp.dot(a,b,preferred_element_type=F32)
def split(x):
    hi=x.astype(BF); return hi,(x-hi.astype(F32)).astype(BF)
def rdot(x,mh,ml):
    h,l=split(x)
    return dot(h,mh)+dot(l,mh)+dot(h,ml)
def ldot(mh,ml,x):
    h,l=split(x)
    return dot(mh,h)+dot(mh,l)+dot(ml,h)

def butterfly(parts, sign):
    (ar,ai),(br,bi),(cr,ci),(dr,di)=parts
    s0r,s0i=ar+cr,ai+ci; s1r,s1i=ar-cr,ai-ci
    t0r,t0i=br+dr,bi+di; t1r,t1i=br-dr,bi-di
    if sign>0: u=(-t1i,t1r)
    else: u=(t1i,-t1r)
    return [(s0r+t0r,s0i+t0i),(s1r+u[0],s1i+u[1]),(s0r-t0r,s0i-t0i),(s1r-u[0],s1i-u[1])]

def layout(rows_dev):
    span=rows_dev+STENCIL-1
    off=max((b*rows_dev)%8 for b in range(8))
    win=-(-(span+off)//8)*8
    return win

def recip_kernel_body(first, nb, rows_dev, n1, n2, pb, win, *refs):
    if first:
        meta,add,kern,mats,twl,tws,out,G,Z,F0,F1=refs
    else:
        meta,vin,kern,mats,twl,tws,out,G,Z,F0,F1=refs
    q2=n2//RADIX; q1=n1//RADIX
    w=2*q2
    def panels(b):
        m=meta[b].astype(F32)
        st=m[2:2+STENCIL*STENCIL]
        lrow=m[18:19]; colq=m[19:20]; colr=m[20:21]
        base=(b*rows_dev)//8*8
        if isinstance(base,int): base=base
        lrow=lrow+(b*rows_dev-base).astype(F32) if rows_dev%8 else lrow
        iq=lax.broadcasted_iota(jnp.int32,(q2,pb),0).astype(F32)
        cols=[jnp.where(colr==float(r),colq,-1.0) for r in range(RADIX)]
        hits=[iq==c for c in cols]
        ir=lax.broadcasted_iota(jnp.int32,(win,pb),0).astype(F32)
        rel=ir-lrow
        rm=[rel==float(a) for a in range(STENCIL)]
        ls=[]
        for b_ in range(STENCIL):
            l=jnp.where(rm[0],st[b_:b_+1],0.0)
            for a in range(1,STENCIL):
                l=jnp.where(rm[a],st[a*STENCIL+b_:a*STENCIL+b_+1],l)
            ls.append(l)
        L=jnp.concatenate(ls,0)
        return m,base,hits,L
    G[...]=jnp.zeros_like(G)
    def spread(b,_):
        m,base,hits,L=panels(b)
        if first:
            vr,vi=m[0:1],m[1:2]
        else:
            v=vin[b].astype(BF).astype(F32); vr,vi=v[0:1],v[1:2]
        ev=[]
        for r in range(RADIX):
            ev.append(jnp.where(hits[r],vr,0.0)); ev.append(jnp.where(hits[r],vi,0.0))
        ev=jnp.concatenate(ev,0).astype(BF)
        S=lax.dot_general(L.astype(BF),ev,(((1,),(1,)),((),())),preferred_element_type=F32)
        start=pl.multiple_of(base,8)
        for r in range(RADIX):
            for c in range(2):
                acc=None
                for b_ in range(STENCIL):
                    rr=(r-b_)%RADIX
                    x=S[b_*win:(b_+1)*win, (rr*2+c)*q2:(rr*2+c+1)*q2]
                    if r-b_<0: x=pltpu.roll(x,1,1)
                    acc=x if acc is None else acc+x
                sl=slice((r*2+c)*q2,(r*2+c+1)*q2)
                G[pl.ds(start,win),sl]=G[pl.ds(start,win),sl]+acc
        return 0
    lax.fori_loop(0,nb,spread,0)
    extra=G.shape[0]-n1
    G[0:extra,:]=G[0:extra,:]+G[n1:n1+extra,:]
    Ah,Al,Bh,Bl=(mats.at[k] for k in range(4))
    ch=128
    def s1(j,_):
        rows=pl.ds(pl.multiple_of(j*ch,ch),ch)
        parts=[]
        for r in range(RADIX):
            y=rdot(G[rows,r*w:(r+1)*w],Ah[...],Al[...])
            re,im=y[:,:q2],y[:,q2:]
            if r:
                c=twl[r,0:1]; s=twl[r,1:2]
                re,im=re*c+im*s, im*c-re*s
            parts.append((re,im))
        for m_,(re,im) in enumerate(butterfly(parts,-1)):
            Z[2*m_,rows,:]=re; Z[2*m_+1,rows,:]=im
        return 0
    lax.fori_loop(0,n1//ch,s1,0)
    def tile2(x): return jnp.concatenate([x,x],1)
    for pair in range(RADIX//2):
        lo=pair*4
        def get(r):
            rr=pl.ds(r,q1,stride=RADIX)
            re=jnp.concatenate([Z[lo,rr,:],Z[lo+2,rr,:]],1)
            im=jnp.concatenate([Z[lo+1,rr,:],Z[lo+3,rr,:]],1)
            return re,im
        parts=[]
        for r in range(RADIX):
            re,im=get(r)
            y=ldot(Bh[...],Bl[...],jnp.concatenate([re,im],0))
            re,im=y[:q1],y[q1:]
            if r:
                c=tile2(tws[r,0]); s=tile2(tws[r,1])
                re,im=re*c+im*s, im*c-re*s
            parts.append((re,im))
        sp=[]
        for m_,(re,im) in enumerate(butterfly(parts,-1)):
            kk=kern[m_*q1:(m_+1)*q1,pair*2*q2:(pair+1)*2*q2]
            sp.append((re*kk,im*kk))
        for r,(re,im) in enumerate(butterfly(sp,1)):
            if r:
                c=tile2(tws[r,0]); s=tile2(tws[r,1])
                re,im=re*c-im*s, im*c+re*s
            y=ldot(Ah[...],Al[...],jnp.concatenate([re,im],0))
            rr=pl.ds(r,q1,stride=RADIX)
            Z[lo,rr,:]=y[:q1,:q2]; Z[lo+2,rr,:]=y[:q1,q2:]
            Z[lo+1,rr,:]=y[q1:,:q2]; Z[lo+3,rr,:]=y[q1:,q2:]
    def s3(j,_):
        rows=pl.ds(pl.multiple_of(j*ch,ch),ch)
        parts=[(Z[2*m_,rows,:],Z[2*m_+1,rows,:]) for m_ in range(RADIX)]
        for r,(re,im) in enumerate(butterfly(parts,1)):
            if r:
                c=twl[r,0:1]; s=twl[r,1:2]
                re,im=re*c-im*s, im*c+re*s
            y=rdot(jnp.concatenate([re,im],1),Bh[...],Bl[...])
            F0[rows,r*w:(r+1)*w]=y
            if r<STENCIL-1:
                F1[rows,r*w:r*w+q2]=pltpu.roll(y[:,:q2],q2-1,1)
                F1[rows,r*w+q2:(r+1)*w]=pltpu.roll(y[:,q2:],q2-1,1)
        return 0
    lax.fori_loop(0,n1//ch,s3,0)
    F0[n1:n1+extra,:]=F0[0:extra,:]
    F1[n1:n1+extra,:]=F1[0:extra,:]
    def gather(b,_):
        m,base,hits,L=panels(b)
        E=jnp.concatenate([jnp.where(h,1.0,0.0) for h in hits],0).astype(BF)
        start=pl.multiple_of(base,8)
        pieces=[]
        for b_ in range(STENCIL):
            for c in range(2):
                blk=[]
                for r in range(RADIX):
                    rr=r+b_
                    src=F0 if rr<RADIX else F1
                    rr%=RADIX
                    blk.append(src[pl.ds(start,win),(rr*2+c)*q2:(rr*2+c+1)*q2])
                pieces.append(jnp.concatenate(blk,1))
        X=jnp.concatenate(pieces,0).astype(BF)
        Pm=dot(X,E)
        for c in range(2):
            acc=None
            for b_ in range(STENCIL):
                x=Pm[(b_*2+c)*win:(b_*2+c+1)*win]*L[b_*win:(b_+1)*win]
                acc=x if acc is None else acc+x
            tot=jnp.sum(acc,0,keepdims=True)
            if first: tot=tot+add[b,c:c+1]
            out[b,c:c+1]=tot
        return 0
    lax.fori_loop(0,nb,gather,0)

def recip(first, meta, other, kern, rows_dev, n1, n2):
    nb=meta.shape[0]; pb=meta.shape[2]
    win=layout(rows_dev)
    mats,tw=tables(n2)
    q=n1//RADIX
    tws=np.ascontiguousarray(np.broadcast_to(tw[:,:,:,None],(RADIX,2,q,n2//RADIX)))
    extra=win
    body=functools.partial(recip_kernel_body,first,nb,rows_dev,n1,n2,pb,win)
    ops=[meta,other]
    return pl.pallas_call(body,
        out_shape=jax.ShapeDtypeStruct((nb,2,pb),F32),
        in_specs=[pl.BlockSpec(memory_space=pltpu.VMEM)]*6,
        out_specs=pl.BlockSpec(memory_space=pltpu.VMEM),
        scratch_shapes=[pltpu.VMEM((n1+extra,2*n2),F32),pltpu.VMEM((2*RADIX,n1,n2//RADIX),F32),pltpu.VMEM((n1+extra,2*n2),F32),pltpu.VMEM((n1+extra,2*n2),F32)],
        compiler_params=pltpu.CompilerParams(vmem_limit_bytes=50*1024*1024),
        cost_estimate=pl.CostEstimate(flops=20_000_000_000,bytes_accessed=8_000_000,transcendentals=0),
        name="recip",
    )(meta,other,kern,jnp.asarray(mats),jnp.asarray(tw),jnp.asarray(tws))


def near_kernel(probes, phase, halo, blocks, source, out, acc):
    step = pl.program_id(0)
    x = halo[0]
    with_real = dot(x, blocks[0, 0])
    with_imag = dot(x, blocks[1, 0])
    real = with_real[:probes] - with_imag[probes:]
    imag = with_real[probes:] + with_imag[:probes]
    c = phase[2 * step]
    s = phase[2 * step + 1]

    @pl.when(step == 0)
    def _():
        acc[...] = 0.5 * source[...]

    acc[0] += real * c - imag * s
    acc[1] += real * s + imag * c

    @pl.when(step == pl.num_programs(0) - 1)
    def _():
        out[:, 0, :] = acc[0]
        out[:, 1, :] = acc[1]


def near_apply(halo, near_blocks, phase, source):
    _, probes, panels = source.shape
    count = near_blocks.shape[1]
    depth = near_blocks.shape[2]
    return pl.pallas_call(
        functools.partial(near_kernel, probes),
        grid=(count,),
        out_shape=jax.ShapeDtypeStruct((probes, 2, panels), F32),
        in_specs=[
            pl.BlockSpec(memory_space=pltpu.SMEM),
            pl.BlockSpec((1, 2 * probes, depth), lambda d: (d, 0, 0)),
            pl.BlockSpec((2, 1, depth, panels), lambda d: (0, d, 0, 0)),
            pl.BlockSpec(source.shape, lambda d: (0, 0, 0)),
        ],
        out_specs=pl.BlockSpec((probes, 2, panels), lambda d: (0, 0, 0)),
        scratch_shapes=[pltpu.VMEM(source.shape, F32)],
        compiler_params=pltpu.CompilerParams(vmem_limit_bytes=16 * 1024 * 1024),
        cost_estimate=pl.CostEstimate(
            flops=4 * count * 2 * probes * depth * panels,
            bytes_accessed=2 * near_blocks.size,
            transcendentals=0,
        ),
        name="near",
    )(phase, halo, near_blocks, source)


def shifted(array, axis, by):
    count = lax.axis_size(axis)
    return lax.ppermute(array, axis, [(i, (i + by) % count) for i in range(count)])


def neighbours(block):
    held = block[None]
    for axis in ("sect", "tile"):
        before = shifted(held, axis, 1)
        after = shifted(held, axis, -1)
        held = jnp.stack([before, held, after])
    return held.reshape((9,) + block.shape)


def phases(bloch_angle):
    tile_pos, tile_count = lax.axis_index("tile"), lax.axis_size("tile")
    sect_pos, sect_count = lax.axis_index("sect"), lax.axis_size("sect")
    offsets = jnp.arange(-1, 2, dtype=jnp.int32)
    leaves_tile = (tile_pos + offsets < 0) | (tile_pos + offsets >= tile_count)
    leaves_sect = (sect_pos + offsets < 0) | (sect_pos + offsets >= sect_count)
    angle_tile = jnp.where(leaves_tile, bloch_angle[0] * offsets, 0.0)
    angle_sect = jnp.where(leaves_sect, bloch_angle[1] * offsets, 0.0)
    angle = (angle_tile[:, None] + angle_sect[None, :]).reshape(9)
    return jnp.stack([jnp.cos(angle), jnp.sin(angle)], axis=1).reshape(18)


def gathered(block):
    for axis in ("sect", "tile"):
        count = lax.axis_size(axis)
        place = lax.axis_index(axis)
        reach = 1
        while reach < count:
            other = lax.ppermute(block, axis, [(i, i ^ reach) for i in range(count)])
            upper = (place // reach) % 2 == 1
            block = jnp.where(
                upper, jnp.concatenate([other, block]), jnp.concatenate([block, other])
            )
            reach *= 2
    return block


def exchange(parts):
    return lax.all_to_all(parts, AXES, 0, 0, tiled=True)


def local(source_probes, near_blocks, bloch_angle, grid_row, grid_col, stencil, recip_kernel):
    count = lax.axis_size("tile") * lax.axis_size("sect")
    n1 = recip_kernel.shape[0]
    n2 = recip_kernel.shape[1] * count
    rows_dev = n1 // count
    _, probes, panels = source_probes.shape
    repeat = count // probes

    def to_owners(rows):
        return jnp.repeat(rows, repeat, axis=0) if repeat > 1 else rows

    def to_panels(rows):
        return exchange(rows)[::repeat]

    rounded = source_probes.astype(BF)
    described = jnp.concatenate(
        [
            stencil.reshape(STENCIL * STENCIL, panels),
            (grid_row % rows_dev)[None].astype(BF),
            (grid_col // RADIX)[None].astype(BF),
            (grid_col % RADIX)[None].astype(BF),
            jnp.zeros((3, panels), BF),
        ]
    )
    sent = jnp.concatenate(
        [
            rounded.transpose(1, 0, 2),
            jnp.broadcast_to(described[None], (probes,) + described.shape),
        ],
        axis=1,
    )
    meta = exchange(to_owners(sent))
    kernel_rows = (recip_kernel * (1.0 / (n1 * n2))).T
    kern = gathered(kernel_rows).T
    phase = phases(bloch_angle)

    def near(source):
        flat = source.astype(BF).reshape(2 * probes, panels)
        return near_apply(neighbours(flat), near_blocks, phase, source)

    start = exchange(to_owners(near(source_probes)))
    first_owned = recip(True, meta, start, kern, rows_dev, n1, n2)
    first_image = to_panels(first_owned).transpose(1, 0, 2)
    second_owned = recip(False, meta, first_owned, kern, rows_dev, n1, n2)
    second_image = (near(first_image) + to_panels(second_owned)).transpose(1, 0, 2)
    return (first_image, second_image)


def solution(mesh):
    return jax.shard_map(
        local,
        mesh=mesh,
        in_specs=(
            P(None, "groups", AXES),
            P("groups", None, None, AXES),
            P("groups"),
            P(AXES),
            P(AXES),
            P(None, None, AXES),
            P("groups", AXES),
        ),
        out_specs=(P(None, "groups", AXES), P(None, "groups", AXES)),
        check_vma=False,
    )
```

```python
import functools

import jax
import jax.numpy as jnp
import ml_dtypes
import numpy as np
from jax import lax
from jax.experimental import pallas as pl
from jax.experimental.pallas import tpu as pltpu
from jax.sharding import PartitionSpec as P

STENCIL = 4
RADIX = 4
UNROLL = 8
F32 = jnp.float32
BF = jnp.bfloat16
AXES = ("tile", "sect")


def split_host(x):
    hi = x.astype(ml_dtypes.bfloat16)
    lo = (x - hi.astype(np.float64)).astype(ml_dtypes.bfloat16)
    return np.stack([hi, lo])


def transform_tables(length):
    short = length // RADIX
    index = np.arange(short)
    tables = []
    for r in range(RADIX):
        angle = 2 * np.pi / length * (((RADIX * index[:, None] + r) * index[None, :]) % length)
        c, s = np.cos(angle), np.sin(angle)
        full = np.block([[c, -s], [s, c]])
        tables.append(np.stack([split_host(full), split_host(full.T)]))
    return np.stack(tables)


def dot(a, b):
    return jnp.dot(a, b, preferred_element_type=F32)


def dot_last(a, b):
    return lax.dot_general(a, b, (((1,), (1,)), ((), ())), preferred_element_type=F32)


def split(x):
    hi = x.astype(BF)
    return hi, (x - hi.astype(F32)).astype(BF)


def times_right(x, table):
    hi, lo = split(x)
    return dot(hi, table[0]) + dot(lo, table[0]) + dot(hi, table[1])


def times_left(table, x):
    hi, lo = split(x)
    return dot(table[0], hi) + dot(table[0], lo) + dot(table[1], hi)


def butterfly(parts, sign):
    (ar, ai), (br, bi), (cr, ci), (dr, di) = parts
    even_r, even_i, diff_r, diff_i = ar + cr, ai + ci, ar - cr, ai - ci
    odd_r, odd_i = br + dr, bi + di
    turn_r, turn_i = (di - bi, br - dr) if sign > 0 else (bi - di, dr - br)
    return [
        (even_r + odd_r, even_i + odd_i),
        (diff_r + turn_r, diff_i + turn_i),
        (even_r - odd_r, even_i - odd_i),
        (diff_r - turn_r, diff_i - turn_i),
    ]


def window_rows(rows_dev):
    lead = max((b * rows_dev) % 8 for b in range(8))
    return -(-(rows_dev + STENCIL - 1 + lead) // 8) * 8


def recip_kernel(rows_dev, n1, n2, meta, scale, tab1, tab2, *rest):
    *source, out, grid, freq, field, ahead = rest
    blocks, _, panels = meta.shape
    q1, q2 = n1 // RADIX, n2 // RADIX
    wide = 2 * q2
    win = window_rows(rows_dev)

    def describe(block):
        rows = meta[block].astype(F32)
        weights = rows[2 : 2 + STENCIL * STENCIL]
        start = (block * rows_dev) // 8 * 8
        first_row = rows[18:19] + (block * rows_dev - start).astype(F32)
        col_group, col_rest = rows[19:20], rows[20:21]
        lane = lax.broadcasted_iota(jnp.int32, (q2, panels), 0).astype(F32)
        hits = [
            jnp.where(lane == jnp.where(col_rest == float(r), col_group, -1.0), 1.0, 0.0)
            for r in range(RADIX)
        ]
        one_hot = jnp.concatenate(hits, 0).astype(BF)
        offset = lax.broadcasted_iota(jnp.int32, (win, panels), 0).astype(F32) - first_row
        at = [offset == float(a) for a in range(STENCIL)]
        spread = []
        for b in range(STENCIL):
            part = jnp.where(at[0], weights[b : b + 1], 0.0)
            for a in range(1, STENCIL):
                k = a * STENCIL + b
                part = jnp.where(at[a], weights[k : k + 1], part)
            spread.append(part)
        return rows, pl.multiple_of(start, 8), one_hot, spread

    grid[...] = jnp.zeros_like(grid)

    def scatter(block, carry):
        rows, start, one_hot, spread = describe(block)
        value = source[0][block].astype(BF).astype(F32) if source else rows[0:2]
        terms = []
        for b in range(STENCIL):
            for c in range(2):
                product = spread[b] * value[c : c + 1]
                hi = product.astype(BF).astype(F32)
                terms += [hi, product - hi]
        sums = dot_last(jnp.concatenate(terms, 0).astype(BF), one_hot)
        for r in range(RADIX):
            for c in range(2):
                total = None
                for b in range(STENCIL):
                    k = (b * 2 + c) * 2 * win
                    lanes = slice((r - b) % RADIX * q2, ((r - b) % RADIX + 1) * q2)
                    x = sums[k : k + win, lanes] + sums[k + win : k + 2 * win, lanes]
                    if r < b:
                        x = pltpu.roll(x, 1, 1)
                    total = x if total is None else total + x
                lanes = slice((r * 2 + c) * q2, (r * 2 + c + 1) * q2)
                grid[pl.ds(start, win), lanes] += total
        return carry

    lax.fori_loop(0, blocks, scatter, 0, unroll=UNROLL)
    grid[0:win, :] += grid[n1 : n1 + win, :]

    parts = []
    for r in range(RADIX):
        y = times_right(grid[0:n1, r * wide : (r + 1) * wide], tab2.at[r, 0])
        parts.append((y[:, :q2], y[:, q2:]))
    for m, (real, imag) in enumerate(butterfly(parts, -1)):
        freq[2 * m] = real
        freq[2 * m + 1] = imag

    for pair in range(0, RADIX, 2):
        parts = []
        for r in range(RADIX):
            rows = pl.ds(r, q1, stride=RADIX)
            both = [
                jnp.concatenate([freq[2 * pair + c, rows, :], freq[2 * pair + 2 + c, rows, :]], 1)
                for c in range(2)
            ]
            y = times_left(tab1.at[r, 1], jnp.concatenate(both, 0))
            parts.append((y[:q1], y[q1:]))
        scaled = []
        for m, (real, imag) in enumerate(butterfly(parts, -1)):
            k = scale[m * q1 : (m + 1) * q1, pair * q2 : (pair + 2) * q2]
            scaled.append((real * k, imag * k))
        for r, both in enumerate(butterfly(scaled, 1)):
            y = times_left(tab1.at[r, 0], jnp.concatenate(both, 0))
            rows = pl.ds(r, q1, stride=RADIX)
            for c in range(2):
                freq[2 * pair + c, rows, :] = y[c * q1 : (c + 1) * q1, :q2]
                freq[2 * pair + 2 + c, rows, :] = y[c * q1 : (c + 1) * q1, q2:]

    parts = [(freq[2 * m], freq[2 * m + 1]) for m in range(RADIX)]
    for r, both in enumerate(butterfly(parts, 1)):
        y = times_right(jnp.concatenate(both, 1), tab2.at[r, 1])
        field[0:n1, r * wide : (r + 1) * wide] = y
        if r < STENCIL - 1:
            for c in range(2):
                lanes = slice((r * 2 + c) * q2, (r * 2 + c + 1) * q2)
                ahead[0:n1, lanes] = pltpu.roll(y[:, c * q2 : (c + 1) * q2], q2 - 1, 1)
    field[n1 : n1 + win, :] = field[0:win, :]
    ahead[n1 : n1 + win, :] = ahead[0:win, :]

    def collect(block, carry):
        _, start, one_hot, spread = describe(block)
        pieces = []
        for b in range(STENCIL):
            for c in range(2):
                row = []
                for r in range(b, b + RADIX):
                    lanes = slice((r % RADIX * 2 + c) * q2, (r % RADIX * 2 + c + 1) * q2)
                    row.append((field if r < RADIX else ahead)[pl.ds(start, win), lanes])
                pieces.append(jnp.concatenate(row, 1))
        values = dot(jnp.concatenate(pieces, 0).astype(BF), one_hot)
        for c in range(2):
            total = None
            for b in range(STENCIL):
                k = (b * 2 + c) * win
                x = values[k : k + win] * spread[b]
                total = x if total is None else total + x
            out[block, c : c + 1] = jnp.sum(total, 0, keepdims=True)
        return carry

    lax.fori_loop(0, blocks, collect, 0, unroll=UNROLL)


def recip_apply(meta, scale, rows_dev, *source):
    blocks, _, panels = meta.shape
    n1, n2 = scale.shape
    reach = n1 + window_rows(rows_dev)
    tab1, tab2 = transform_tables(n1), transform_tables(n2)
    in_vmem = pl.BlockSpec(memory_space=pltpu.VMEM)
    return pl.pallas_call(
        functools.partial(recip_kernel, rows_dev, n1, n2),
        out_shape=jax.ShapeDtypeStruct((blocks, 2, panels), F32),
        in_specs=[in_vmem] * (4 + len(source)),
        out_specs=in_vmem,
        scratch_shapes=[
            pltpu.VMEM((reach, 2 * n2), F32),
            pltpu.VMEM((2 * RADIX, n1, n2 // RADIX), F32),
            pltpu.VMEM((reach, 2 * n2), F32),
            pltpu.VMEM((reach, 2 * n2 // RADIX * (STENCIL - 1)), F32),
        ],
        compiler_params=pltpu.CompilerParams(vmem_limit_bytes=28 * 1024 * 1024),
        cost_estimate=pl.CostEstimate(
            flops=10_000_000_000, bytes_accessed=8_000_000, transcendentals=0
        ),
        name="recip",
    )(meta, scale, jnp.asarray(tab1), jnp.asarray(tab2), *source)


def border_phases(bloch):
    lane = lax.broadcasted_iota(jnp.int32, (1, 128), 1)
    angle = jnp.zeros((1, 128), F32)
    for k, (axis, offset) in enumerate(zip(AXES, (lane // 3 - 1, lane % 3 - 1))):
        place = lax.axis_index(axis) + offset
        leaves = (place < 0) | (place >= lax.axis_size(axis))
        angle += jnp.where(leaves, bloch[k] * offset.astype(F32), 0.0)
    return jnp.cos(angle), jnp.sin(angle)


def near_kernel(probes_first, bloch, halo, source, blocks, out):
    count, twice, _ = halo.shape
    probes = twice // 2
    cosines, sines = border_phases(bloch)
    total_real = 0.5 * source[0]
    total_imag = 0.5 * source[1]
    for d in range(count):
        x = halo[d]
        with_real = dot(x, blocks[0, d])
        with_imag = dot(x, blocks[1, d])
        real = with_real[:probes] - with_imag[probes:]
        imag = with_real[probes:] + with_imag[:probes]
        c = cosines[:, d : d + 1]
        s = sines[:, d : d + 1]
        total_real += real * c - imag * s
        total_imag += real * s + imag * c
    for c, total in enumerate((total_real, total_imag)):
        if probes_first:
            out[:, c, :] = total
        else:
            out[c] = total


def near_apply(halo, near_blocks, bloch_angle, source, probes_first):
    _, probes, panels = source.shape
    _, count, depth, _ = near_blocks.shape
    in_vmem = pl.BlockSpec(memory_space=pltpu.VMEM)
    shape = (probes, 2, panels) if probes_first else (2, probes, panels)
    return pl.pallas_call(
        functools.partial(near_kernel, probes_first),
        out_shape=jax.ShapeDtypeStruct(shape, F32),
        in_specs=[pl.BlockSpec(memory_space=pltpu.SMEM), in_vmem, in_vmem, in_vmem],
        out_specs=in_vmem,
        compiler_params=pltpu.CompilerParams(vmem_limit_bytes=8 * 1024 * 1024),
        cost_estimate=pl.CostEstimate(
            flops=4 * count * 2 * probes * depth * panels,
            bytes_accessed=2 * near_blocks.size,
            transcendentals=0,
        ),
        name="near",
    )(bloch_angle, halo, source, near_blocks)


def neighbour_kernel(tiles, sects, part, start, image, sent):
    image[...] = part[...] + start[...]

    def lay(block, carry):
        tile, sect = block // sects, block % sects
        rows = []
        for d in (-1, 0, 1):
            for e in (-1, 0, 1):
                near = (tile + d + tiles) % tiles * sects + (sect + e + sects) % sects
                rows.append(image[near])
        mine = image[block]
        hi = mine.astype(BF).astype(F32)
        mid = (mine - hi).astype(BF).astype(F32)
        rows += [mid, mine - hi - mid, jnp.zeros_like(mine)]
        sent[block] = jnp.concatenate(rows, 0).astype(BF)
        return carry

    lax.fori_loop(0, image.shape[0], lay, 0, unroll=4)


def neighbour_rows(part, start):
    blocks, _, panels = part.shape
    in_vmem = pl.BlockSpec(memory_space=pltpu.VMEM)
    return pl.pallas_call(
        functools.partial(neighbour_kernel, lax.axis_size("tile"), lax.axis_size("sect")),
        out_shape=(
            jax.ShapeDtypeStruct(part.shape, F32),
            jax.ShapeDtypeStruct((blocks, 24, panels), BF),
        ),
        in_specs=[in_vmem] * 2,
        out_specs=(in_vmem, in_vmem),
        compiler_params=pltpu.CompilerParams(vmem_limit_bytes=24 * 1024 * 1024),
        name="neighbour_rows",
    )(part, start)


def pack_kernel(rows_dev, source, stencil, first_row, first_col, sent, low):
    probes, panels = source.shape[1:]
    row, col = first_row[...], first_col[...]
    numbers = [row % rows_dev, col // RADIX, col % RADIX]
    rows = [stencil[a].astype(F32) for a in range(STENCIL)] + [x.astype(F32) for x in numbers]
    rows.append(jnp.zeros((3, panels), F32))
    described = jnp.concatenate(rows, 0)
    for p in range(probes):
        value = [source[c, p : p + 1, :] for c in range(2)]
        sent[p] = jnp.concatenate(value + [described], 0).astype(BF)
    for c in range(2):
        low[c * probes : (c + 1) * probes] = source[c].astype(BF)


def pack(rows_dev, source, stencil, grid_row, grid_col):
    _, probes, panels = source.shape
    rows = 2 + STENCIL * STENCIL + 6
    in_vmem = pl.BlockSpec(memory_space=pltpu.VMEM)
    return pl.pallas_call(
        functools.partial(pack_kernel, rows_dev),
        out_shape=(
            jax.ShapeDtypeStruct((probes, rows, panels), BF),
            jax.ShapeDtypeStruct((2 * probes, panels), BF),
        ),
        in_specs=[in_vmem] * 4,
        out_specs=(in_vmem, in_vmem),
        compiler_params=pltpu.CompilerParams(vmem_limit_bytes=16 * 1024 * 1024),
        name="pack",
    )(source, stencil, grid_row[None], grid_col[None])


def shifted(array, axis, by):
    count = lax.axis_size(axis)
    return lax.ppermute(array, axis, [(i, (i + by) % count) for i in range(count)])


def beside(block, axis):
    return jnp.stack([shifted(block, axis, 1), block, shifted(block, axis, -1)])


def doubling_steps():
    far = [(axis, 2**p) for axis in AXES[::-1] for p in range(1, 12) if 2**p < lax.axis_size(axis)]
    return far[::-1] + [(axis, 1) for axis in AXES[::-1] if lax.axis_size(axis) > 1]


def doubled(block, step):
    axis, reach = step
    other = lax.ppermute(block, axis, [(i, i ^ reach) for i in range(lax.axis_size(axis))])
    upper = (lax.axis_index(axis) // reach) % 2 == 1
    return jnp.where(upper, jnp.stack([other, block]), jnp.stack([block, other]))


def in_columns(block, steps):
    held = steps[::-1]
    order = sorted(range(len(held)), key=lambda k: (AXES.index(held[k][0]), -held[k][1]))
    *_, columns, length = block.shape
    dims = len(held)
    whole = block.transpose([dims + 1] + order + [dims])
    return whole.reshape(length, columns * 2**dims)


def exchange(parts):
    return lax.all_to_all(parts, AXES, 0, 0, tiled=True)


def local(source_probes, near_blocks, bloch_angle, grid_row, grid_col, stencil, recip_kernel):
    count = lax.axis_size("tile") * lax.axis_size("sect")
    n1 = recip_kernel.shape[0]
    n2 = recip_kernel.shape[1] * count
    rows_dev = n1 // count
    _, probes, panels = source_probes.shape
    repeat = count // probes

    def to_owners(rows):
        return jnp.repeat(rows, repeat, axis=0) if repeat > 1 else rows

    def to_panels(rows):
        return exchange(rows)[::repeat]

    sent, low = pack(rows_dev, source_probes, stencil, grid_row, grid_col)
    meta = exchange(to_owners(sent))
    steps = doubling_steps()
    kernel_rows = doubled((recip_kernel * (1.0 / (n1 * n2))).T, steps[0])
    kernel_rows, low = lax.optimization_barrier((kernel_rows, low))
    halo = beside(beside(low, "sect"), "tile").reshape(9, 2 * probes, panels)
    for step in steps[1:-1]:
        kernel_rows = doubled(kernel_rows, step)
    first_near = near_apply(halo, near_blocks, bloch_angle, source_probes, True)
    kernel_rows, first_near = lax.optimization_barrier((kernel_rows, first_near))
    scale = in_columns(doubled(kernel_rows, steps[-1]), steps)
    start = exchange(to_owners(first_near))
    first_owned, spread = neighbour_rows(recip_apply(meta, scale, rows_dev), start)
    second_owned = recip_apply(meta, scale, rows_dev, first_owned)
    rows, second_owned = lax.optimization_barrier((to_panels(spread), second_owned))
    rows = rows.transpose(1, 0, 2)
    halo = rows[:18].reshape(9, 2 * probes, panels)
    first_image = rows[8:10].astype(F32) + rows[18:20].astype(F32) + rows[20:22].astype(F32)
    second_near = near_apply(halo, near_blocks, bloch_angle, first_image, False)
    second_image = second_near + to_panels(second_owned).transpose(1, 0, 2)
    return (first_image, second_image)


def solution(mesh):
    return jax.shard_map(
        local,
        mesh=mesh,
        in_specs=(
            P(None, "groups", AXES),
            P("groups", None, None, AXES),
            P("groups"),
            P(AXES),
            P(AXES),
            P(None, None, AXES),
            P("groups", AXES),
        ),
        out_specs=(P(None, "groups", AXES), P(None, "groups", AXES)),
        check_vma=False,
    )
```

```python
import functools

import jax
import jax.numpy as jnp
import ml_dtypes
import numpy as np
from jax import lax
from jax.experimental import pallas as pl
from jax.experimental.pallas import tpu as pltpu
from jax.sharding import PartitionSpec as P

STENCIL = 4
RADIX = 4
UNROLL = 16
MOST_HELD = 20 * 1024 * 1024
F32 = jnp.float32
BF = jnp.bfloat16
AXES = ("tile", "sect")


def split_host(x):
    hi = x.astype(ml_dtypes.bfloat16)
    lo = (x - hi.astype(np.float64)).astype(ml_dtypes.bfloat16)
    return np.stack([hi, lo])


def transform_tables(length):
    short = length // RADIX
    index = np.arange(short)
    tables = []
    for r in range(RADIX):
        angle = 2 * np.pi / length * (((RADIX * index[:, None] + r) * index[None, :]) % length)
        c, s = np.cos(angle), np.sin(angle)
        full = np.block([[c, -s], [s, c]])
        tables.append(np.stack([split_host(full), split_host(full.T)]))
    return np.stack(tables)


def dot(a, b):
    return jnp.dot(a, b, preferred_element_type=F32)


def dot_last(a, b):
    return lax.dot_general(a, b, (((1,), (1,)), ((), ())), preferred_element_type=F32)


def split(x):
    hi = x.astype(BF)
    return hi, (x - hi.astype(F32)).astype(BF)


def times_right(x, table):
    hi, lo = split(x)
    rows = x.shape[0]
    y = dot(jnp.concatenate([hi, lo], 0), table[0])
    return y[:rows] + y[rows:] + dot(hi, table[1])


def times_left(table, x):
    hi, lo = split(x)
    rows = x.shape[0]
    y = dot(table[...].reshape(2 * rows, rows), hi)
    return y[:rows] + y[rows:] + dot(table[0], lo)


def butterfly(parts, sign):
    (ar, ai), (br, bi), (cr, ci), (dr, di) = parts
    even_r, even_i, diff_r, diff_i = ar + cr, ai + ci, ar - cr, ai - ci
    odd_r, odd_i = br + dr, bi + di
    turn_r, turn_i = (di - bi, br - dr) if sign > 0 else (bi - di, dr - br)
    return [
        (even_r + odd_r, even_i + odd_i),
        (diff_r + turn_r, diff_i + turn_i),
        (even_r - odd_r, even_i - odd_i),
        (diff_r - turn_r, diff_i - turn_i),
    ]


def window_rows(rows_dev):
    lead = max((b * rows_dev) % 8 for b in range(8))
    return -(-(rows_dev + STENCIL - 1 + lead) // 8) * 8


def held_bytes(shape, rows_dev, n2):
    blocks, _, panels = shape
    return blocks * panels * RADIX * (2 * (n2 // RADIX) + 4 * window_rows(rows_dev))


def recip_kernel(rows_dev, n1, n2, meta, scale, tab1, tab2, *rest):
    keep = held_bytes(meta.shape, rows_dev, n2) <= MOST_HELD
    *source, out, grid, freq = rest[: len(rest) - 2 * keep]
    hot, weight = rest[len(rest) - 2 :]
    blocks, _, panels = meta.shape
    q1, q2 = n1 // RADIX, n2 // RADIX
    wide = 2 * q2
    win = window_rows(rows_dev)

    def start_of(block):
        return pl.multiple_of((block * rows_dev) // 8 * 8, 8)

    grid[...] = jnp.zeros_like(grid)

    def describe(block):
        rows = meta[block].astype(F32)
        offset = lax.broadcasted_iota(jnp.int32, (win, panels), 0).astype(F32)
        offset = offset - (rows[18:19] + (block * rows_dev - start_of(block)).astype(F32))
        at = [offset == float(a) for a in range(STENCIL)]
        lane = lax.broadcasted_iota(jnp.int32, (q2, panels), 0).astype(F32)
        for r in range(RADIX):
            spread = jnp.zeros((win, panels), F32)
            for a in range(STENCIL):
                k = 2 + a * RADIX + r
                spread = jnp.where(at[a], rows[k : k + 1], spread)
            one_hot = jnp.where(lane == rows[19 + r : 20 + r], 1.0, 0.0).astype(BF)
            yield r, spread, one_hot

    def scatter(block, carry):
        value = source[0][block].astype(BF).astype(F32) if source else meta[block].astype(F32)[0:2]
        start = start_of(block)
        for r, spread, one_hot in describe(block):
            if keep:
                weight[block, r] = spread
                hot[block, r] = one_hot
            both = jnp.concatenate([spread * value[c : c + 1] for c in range(2)], 0)
            sums = dot_last(jnp.concatenate(split(both), 0), one_hot)
            sums = sums[: 2 * win] + sums[2 * win :]
            for c in range(2):
                lanes = slice((r * 2 + c) * q2, (r * 2 + c + 1) * q2)
                grid[pl.ds(start, win), lanes] += sums[c * win : (c + 1) * win]
        return carry

    lax.fori_loop(0, blocks, scatter, 0, unroll=UNROLL)
    grid[0:win, :] += grid[n1 : n1 + win, :]

    parts = []
    for r in range(RADIX):
        y = times_right(grid[0:n1, r * wide : (r + 1) * wide], tab2.at[r, 0])
        parts.append((y[:, :q2], y[:, q2:]))
    for m, (real, imag) in enumerate(butterfly(parts, -1)):
        freq[2 * m] = real
        freq[2 * m + 1] = imag

    for pair in range(0, RADIX, 2):
        parts = []
        for r in range(RADIX):
            rows = pl.ds(r, q1, stride=RADIX)
            both = [
                jnp.concatenate([freq[2 * pair + c, rows, :], freq[2 * pair + 2 + c, rows, :]], 1)
                for c in range(2)
            ]
            y = times_left(tab1.at[r, 1], jnp.concatenate(both, 0))
            parts.append((y[:q1], y[q1:]))
        scaled = []
        for m, (real, imag) in enumerate(butterfly(parts, -1)):
            k = scale[m * q1 : (m + 1) * q1, pair * q2 : (pair + 2) * q2]
            scaled.append((real * k, imag * k))
        for r, both in enumerate(butterfly(scaled, 1)):
            y = times_left(tab1.at[r, 0], jnp.concatenate(both, 0))
            rows = pl.ds(r, q1, stride=RADIX)
            for c in range(2):
                freq[2 * pair + c, rows, :] = y[c * q1 : (c + 1) * q1, :q2]
                freq[2 * pair + 2 + c, rows, :] = y[c * q1 : (c + 1) * q1, q2:]

    parts = [(freq[2 * m], freq[2 * m + 1]) for m in range(RADIX)]
    for r, both in enumerate(butterfly(parts, 1)):
        grid[0:n1, r * wide : (r + 1) * wide] = times_right(jnp.concatenate(both, 1), tab2.at[r, 1])
    grid[n1 : n1 + win, :] = grid[0:win, :]

    def held(block):
        for r in range(RADIX):
            yield r, weight[block, r], hot[block, r]

    def collect(block, carry):
        start = start_of(block)
        totals = [jnp.zeros((win, panels), F32)] * 2
        for r, spread, one_hot in held(block) if keep else describe(block):
            near = [grid[pl.ds(start, win), (r * 2 + c) * q2 : (r * 2 + c + 1) * q2] for c in range(2)]
            values = dot(jnp.concatenate(near, 0).astype(BF), one_hot)
            for c in range(2):
                totals[c] = totals[c] + values[c * win : (c + 1) * win] * spread
        for c in range(2):
            out[block, c : c + 1] = jnp.sum(totals[c], 0, keepdims=True)
        return carry

    lax.fori_loop(0, blocks, collect, 0, unroll=UNROLL)


def recip_apply(meta, scale, rows_dev, *source):
    blocks, _, panels = meta.shape
    n1, n2 = scale.shape
    reach = n1 + window_rows(rows_dev)
    kept = [
        pltpu.VMEM((blocks, RADIX, n2 // RADIX, panels), BF),
        pltpu.VMEM((blocks, RADIX, window_rows(rows_dev), panels), F32),
    ]
    if held_bytes(meta.shape, rows_dev, n2) > MOST_HELD:
        kept = []
    tab1, tab2 = transform_tables(n1), transform_tables(n2)
    in_vmem = pl.BlockSpec(memory_space=pltpu.VMEM)
    return pl.pallas_call(
        functools.partial(recip_kernel, rows_dev, n1, n2),
        out_shape=jax.ShapeDtypeStruct((blocks, 2, panels), F32),
        in_specs=[in_vmem] * (4 + len(source)),
        out_specs=in_vmem,
        scratch_shapes=[
            pltpu.VMEM((reach, 2 * n2), F32),
            pltpu.VMEM((2 * RADIX, n1, n2 // RADIX), F32),
        ]
        + kept,
        compiler_params=pltpu.CompilerParams(vmem_limit_bytes=40 * 1024 * 1024),
        cost_estimate=pl.CostEstimate(
            flops=10_000_000_000, bytes_accessed=8_000_000, transcendentals=0
        ),
        name="recip",
    )(meta, scale, jnp.asarray(tab1), jnp.asarray(tab2), *source)


def border_phases(bloch):
    lane = lax.broadcasted_iota(jnp.int32, (1, 128), 1)
    angle = jnp.zeros((1, 128), F32)
    for k, (axis, offset) in enumerate(zip(AXES, (lane // 3 - 1, lane % 3 - 1))):
        place = lax.axis_index(axis) + offset
        leaves = (place < 0) | (place >= lax.axis_size(axis))
        angle += jnp.where(leaves, bloch[k] * offset.astype(F32), 0.0)
    return jnp.cos(angle), jnp.sin(angle)


def near_kernel(probes_first, bloch, halo, source, blocks, out):
    count, twice, _ = halo.shape
    probes = twice // 2
    cosines, sines = border_phases(bloch)
    total_real = 0.5 * source[0]
    total_imag = 0.5 * source[1]
    for d in range(count):
        x = halo[d]
        with_real = dot(x, blocks[0, d])
        with_imag = dot(x, blocks[1, d])
        real = with_real[:probes] - with_imag[probes:]
        imag = with_real[probes:] + with_imag[:probes]
        c = cosines[:, d : d + 1]
        s = sines[:, d : d + 1]
        total_real += real * c - imag * s
        total_imag += real * s + imag * c
    for c, total in enumerate((total_real, total_imag)):
        if probes_first:
            out[:, c, :] = total
        else:
            out[c] = total


def near_apply(halo, near_blocks, bloch_angle, source, probes_first):
    _, probes, panels = source.shape
    _, count, depth, _ = near_blocks.shape
    in_vmem = pl.BlockSpec(memory_space=pltpu.VMEM)
    shape = (probes, 2, panels) if probes_first else (2, probes, panels)
    return pl.pallas_call(
        functools.partial(near_kernel, probes_first),
        out_shape=jax.ShapeDtypeStruct(shape, F32),
        in_specs=[pl.BlockSpec(memory_space=pltpu.SMEM), in_vmem, in_vmem, in_vmem],
        out_specs=in_vmem,
        compiler_params=pltpu.CompilerParams(vmem_limit_bytes=8 * 1024 * 1024),
        cost_estimate=pl.CostEstimate(
            flops=4 * count * 2 * probes * depth * panels,
            bytes_accessed=2 * near_blocks.size,
            transcendentals=0,
        ),
        name="near",
    )(bloch_angle, halo, source, near_blocks)


def neighbour_kernel(tiles, sects, part, start, image, sent):
    image[...] = part[...] + start[...]

    def lay(block, carry):
        tile, sect = block // sects, block % sects
        rows = []
        for d in (-1, 0, 1):
            for e in (-1, 0, 1):
                near = (tile + d + tiles) % tiles * sects + (sect + e + sects) % sects
                rows.append(image[near])
        mine = image[block]
        hi = mine.astype(BF).astype(F32)
        mid = (mine - hi).astype(BF).astype(F32)
        rows += [mid, mine - hi - mid, jnp.zeros_like(mine)]
        sent[block] = jnp.concatenate(rows, 0).astype(BF)
        return carry

    lax.fori_loop(0, image.shape[0], lay, 0, unroll=4)


def neighbour_rows(part, start):
    blocks, _, panels = part.shape
    in_vmem = pl.BlockSpec(memory_space=pltpu.VMEM)
    return pl.pallas_call(
        functools.partial(neighbour_kernel, lax.axis_size("tile"), lax.axis_size("sect")),
        out_shape=(
            jax.ShapeDtypeStruct(part.shape, F32),
            jax.ShapeDtypeStruct((blocks, 24, panels), BF),
        ),
        in_specs=[in_vmem] * 2,
        out_specs=(in_vmem, in_vmem),
        compiler_params=pltpu.CompilerParams(vmem_limit_bytes=24 * 1024 * 1024),
        name="neighbour_rows",
    )(part, start)


def pack_kernel(rows_dev, groups, *refs):
    given, (sent, low), held, sems = refs[:4], refs[4:6], refs[6:10], refs[10]
    copies = [pltpu.make_async_copy(given[k], held[k], sems.at[k]) for k in range(4)]
    for copy in copies:
        copy.start()
    for copy in copies:
        copy.wait()
    source, stencil, first_row, first_col = held
    probes, panels = source.shape[1:]
    row, col = first_row[...], first_col[...]
    rest = col % RADIX
    given = [stencil[a].astype(F32) for a in range(STENCIL)]
    rows = []
    for a in range(STENCIL):
        for r in range(RADIX):
            taken = given[a][r : r + 1]
            for k in range(1, RADIX):
                b = (r - k) % RADIX
                taken = jnp.where(rest == k, given[a][b : b + 1], taken)
            rows.append(taken)
    rows.append((row % rows_dev).astype(F32))
    for r in range(RADIX):
        group = col // RADIX + jnp.where(rest > r, 1, 0)
        rows.append(jnp.where(group == groups, 0, group).astype(F32))
    rows.append(jnp.zeros((1, panels), F32))
    described = jnp.concatenate(rows, 0)
    for p in range(probes):
        value = [source[c, p : p + 1, :] for c in range(2)]
        sent[p] = jnp.concatenate(value + [described], 0).astype(BF)
    for c in range(2):
        low[c * probes : (c + 1) * probes] = source[c].astype(BF)


def pack(rows_dev, n2, source, stencil, grid_row, grid_col):
    _, probes, panels = source.shape
    rows = 2 + STENCIL * RADIX + 6
    in_vmem = pl.BlockSpec(memory_space=pltpu.VMEM)
    given = (source, stencil, grid_row[None], grid_col[None])
    return pl.pallas_call(
        functools.partial(pack_kernel, rows_dev, n2 // RADIX),
        out_shape=(
            jax.ShapeDtypeStruct((probes, rows, panels), BF),
            jax.ShapeDtypeStruct((2 * probes, panels), BF),
        ),
        in_specs=[pl.BlockSpec(memory_space=pl.ANY)] * 4,
        out_specs=(in_vmem, in_vmem),
        scratch_shapes=[pltpu.VMEM(x.shape, x.dtype) for x in given] + [pltpu.SemaphoreType.DMA((4,))],
        compiler_params=pltpu.CompilerParams(vmem_limit_bytes=60 * 1024 * 1024),
        name="pack",
    )(*given)


def shifted(array, axis, by):
    count = lax.axis_size(axis)
    return lax.ppermute(array, axis, [(i, (i + by) % count) for i in range(count)])


def beside(block, axis):
    return jnp.stack([shifted(block, axis, 1), block, shifted(block, axis, -1)])


def doubling_steps():
    far = [(axis, 2**p) for axis in AXES[::-1] for p in range(1, 12) if 2**p < lax.axis_size(axis)]
    return far[::-1] + [(axis, 1) for axis in AXES[::-1] if lax.axis_size(axis) > 1]


def doubled(block, step):
    axis, reach = step
    other = lax.ppermute(block, axis, [(i, i ^ reach) for i in range(lax.axis_size(axis))])
    upper = (lax.axis_index(axis) // reach) % 2 == 1
    return jnp.where(upper, jnp.stack([other, block]), jnp.stack([block, other]))


def in_columns(block, steps):
    held = steps[::-1]
    order = sorted(range(len(held)), key=lambda k: (AXES.index(held[k][0]), -held[k][1]))
    *_, columns, length = block.shape
    dims = len(held)
    whole = block.transpose([dims + 1] + order + [dims])
    return whole.reshape(length, columns * 2**dims)


def exchange(parts):
    return lax.all_to_all(parts, AXES, 0, 0, tiled=True)


def local(source_probes, near_blocks, bloch_angle, grid_row, grid_col, stencil, recip_kernel):
    count = lax.axis_size("tile") * lax.axis_size("sect")
    n1 = recip_kernel.shape[0]
    n2 = recip_kernel.shape[1] * count
    rows_dev = n1 // count
    _, probes, panels = source_probes.shape
    repeat = count // probes

    def to_owners(rows):
        return jnp.repeat(rows, repeat, axis=0) if repeat > 1 else rows

    def to_panels(rows):
        return exchange(rows)[::repeat]

    sent, low = pack(rows_dev, n2, source_probes, stencil, grid_row, grid_col)
    meta = exchange(to_owners(sent))
    steps = doubling_steps()
    kernel_rows = doubled((recip_kernel * (1.0 / (n1 * n2))).T, steps[0])
    kernel_rows, low = lax.optimization_barrier((kernel_rows, low))
    halo = beside(beside(low, "sect"), "tile").reshape(9, 2 * probes, panels)
    for step in steps[1:-1]:
        kernel_rows = doubled(kernel_rows, step)
    kernel_rows, halo = lax.optimization_barrier((kernel_rows, halo))
    scale = in_columns(doubled(kernel_rows, steps[-1]), steps)
    first_near = near_apply(halo, near_blocks, bloch_angle, source_probes, True)
    start = exchange(to_owners(first_near))
    first_owned, spread = neighbour_rows(recip_apply(meta, scale, rows_dev), start)
    second_owned = recip_apply(meta, scale, rows_dev, first_owned)
    rows, second_owned = lax.optimization_barrier((to_panels(spread), second_owned))
    rows = rows.transpose(1, 0, 2)
    halo = rows[:18].reshape(9, 2 * probes, panels)
    first_image = rows[8:10].astype(F32) + rows[18:20].astype(F32) + rows[20:22].astype(F32)
    second_near = near_apply(halo, near_blocks, bloch_angle, first_image, False)
    second_image = second_near + to_panels(second_owned).transpose(1, 0, 2)
    return (first_image, second_image)


def solution(mesh):
    return jax.shard_map(
        local,
        mesh=mesh,
        in_specs=(
            P(None, "groups", AXES),
            P("groups", None, None, AXES),
            P("groups"),
            P(AXES),
            P(AXES),
            P(None, None, AXES),
            P("groups", AXES),
        ),
        out_specs=(P(None, "groups", AXES), P(None, "groups", AXES)),
        check_vma=False,
    )
```

```python
import functools

import jax
import jax.numpy as jnp
import ml_dtypes
import numpy as np
from jax import lax
from jax.experimental import pallas as pl
from jax.experimental.pallas import tpu as pltpu
from jax.sharding import PartitionSpec as P

STENCIL = 4
RADIX = 4
UNROLL = 16
MOST_HELD = 20 * 1024 * 1024
F32 = jnp.float32
BF = jnp.bfloat16
AXES = ("tile", "sect")


def split_host(x):
    hi = x.astype(ml_dtypes.bfloat16)
    lo = (x - hi.astype(np.float64)).astype(ml_dtypes.bfloat16)
    return np.stack([hi, lo])


def transform_tables(length):
    short = length // RADIX
    index = np.arange(short)
    tables = []
    for r in range(RADIX):
        angle = 2 * np.pi / length * (((RADIX * index[:, None] + r) * index[None, :]) % length)
        c, s = np.cos(angle), np.sin(angle)
        full = np.block([[c, -s], [s, c]])
        tables.append(np.stack([split_host(full), split_host(full.T)]))
    return np.stack(tables)


def dot(a, b):
    return jnp.dot(a, b, preferred_element_type=F32)


def dot_last(a, b):
    return lax.dot_general(a, b, (((1,), (1,)), ((), ())), preferred_element_type=F32)


def split(x):
    hi = x.astype(BF)
    return hi, (x - hi.astype(F32)).astype(BF)


def times_right(x, table):
    hi, lo = split(x)
    rows = x.shape[0]
    y = dot(jnp.concatenate([hi, lo], 0), table[0])
    return y[:rows] + y[rows:] + dot(hi, table[1])


def times_left(table, x):
    hi, lo = split(x)
    rows = x.shape[0]
    y = dot(table[...].reshape(2 * rows, rows), hi)
    return y[:rows] + y[rows:] + dot(table[0], lo)


def butterfly(parts, sign):
    (ar, ai), (br, bi), (cr, ci), (dr, di) = parts
    even_r, even_i, diff_r, diff_i = ar + cr, ai + ci, ar - cr, ai - ci
    odd_r, odd_i = br + dr, bi + di
    turn_r, turn_i = (di - bi, br - dr) if sign > 0 else (bi - di, dr - br)
    return [
        (even_r + odd_r, even_i + odd_i),
        (diff_r + turn_r, diff_i + turn_i),
        (even_r - odd_r, even_i - odd_i),
        (diff_r - turn_r, diff_i - turn_i),
    ]


def window_rows(rows_dev):
    lead = max((b * rows_dev) % 8 for b in range(8))
    return -(-(rows_dev + STENCIL - 1 + lead) // 8) * 8


def held_bytes(shape, rows_dev, n2):
    blocks, _, panels = shape
    return blocks * panels * RADIX * (2 * (n2 // RADIX) + 4 * window_rows(rows_dev))


def recip_kernel(rows_dev, n1, n2, meta, scale, tab1, tab2, *rest):
    keep = held_bytes(meta.shape, rows_dev, n2) <= MOST_HELD
    *source, out, grid, freq = rest[: len(rest) - 2 * keep]
    hot, weight = rest[len(rest) - 2 :]
    blocks, _, panels = meta.shape
    q1, q2 = n1 // RADIX, n2 // RADIX
    wide = 2 * q2
    win = window_rows(rows_dev)

    def start_of(block):
        return pl.multiple_of((block * rows_dev) // 8 * 8, 8)

    grid[...] = jnp.zeros_like(grid)

    def describe(block):
        rows = meta[block].astype(F32)
        offset = lax.broadcasted_iota(jnp.int32, (win, panels), 0).astype(F32)
        offset = offset - (rows[18:19] + (block * rows_dev - start_of(block)).astype(F32))
        at = [offset == float(a) for a in range(STENCIL)]
        lane = lax.broadcasted_iota(jnp.int32, (q2, panels), 0).astype(F32)
        for r in range(RADIX):
            spread = jnp.zeros((win, panels), F32)
            for a in range(STENCIL):
                k = 2 + a * RADIX + r
                spread = jnp.where(at[a], rows[k : k + 1], spread)
            one_hot = jnp.where(lane == rows[19 + r : 20 + r], 1.0, 0.0).astype(BF)
            yield r, spread, one_hot

    def scatter(block, carry):
        value = source[0][block].astype(BF).astype(F32) if source else meta[block].astype(F32)[0:2]
        start = start_of(block)
        for r, spread, one_hot in describe(block):
            if keep:
                weight[block, r] = spread
                hot[block, r] = one_hot
            both = jnp.concatenate([spread * value[c : c + 1] for c in range(2)], 0)
            sums = dot_last(jnp.concatenate(split(both), 0), one_hot)
            sums = sums[: 2 * win] + sums[2 * win :]
            for c in range(2):
                lanes = slice((r * 2 + c) * q2, (r * 2 + c + 1) * q2)
                grid[pl.ds(start, win), lanes] += sums[c * win : (c + 1) * win]
        return carry

    lax.fori_loop(0, blocks, scatter, 0, unroll=UNROLL)
    grid[0:win, :] += grid[n1 : n1 + win, :]

    parts = []
    for r in range(RADIX):
        y = times_right(grid[0:n1, r * wide : (r + 1) * wide], tab2.at[r, 0])
        parts.append((y[:, :q2], y[:, q2:]))
    for m, (real, imag) in enumerate(butterfly(parts, -1)):
        freq[2 * m] = real
        freq[2 * m + 1] = imag

    for pair in range(0, RADIX, 2):
        parts = []
        for r in range(RADIX):
            rows = pl.ds(r, q1, stride=RADIX)
            both = [
                jnp.concatenate([freq[2 * pair + c, rows, :], freq[2 * pair + 2 + c, rows, :]], 1)
                for c in range(2)
            ]
            y = times_left(tab1.at[r, 1], jnp.concatenate(both, 0))
            parts.append((y[:q1], y[q1:]))
        scaled = []
        for m, (real, imag) in enumerate(butterfly(parts, -1)):
            k = scale[m * q1 : (m + 1) * q1, pair * q2 : (pair + 2) * q2]
            scaled.append((real * k, imag * k))
        for r, both in enumerate(butterfly(scaled, 1)):
            y = times_left(tab1.at[r, 0], jnp.concatenate(both, 0))
            rows = pl.ds(r, q1, stride=RADIX)
            for c in range(2):
                freq[2 * pair + c, rows, :] = y[c * q1 : (c + 1) * q1, :q2]
                freq[2 * pair + 2 + c, rows, :] = y[c * q1 : (c + 1) * q1, q2:]

    parts = [(freq[2 * m], freq[2 * m + 1]) for m in range(RADIX)]
    for r, both in enumerate(butterfly(parts, 1)):
        grid[0:n1, r * wide : (r + 1) * wide] = times_right(jnp.concatenate(both, 1), tab2.at[r, 1])
    grid[n1 : n1 + win, :] = grid[0:win, :]

    def held(block):
        for r in range(RADIX):
            yield r, weight[block, r], hot[block, r]

    def collect(block, carry):
        start = start_of(block)
        totals = [jnp.zeros((win, panels), F32)] * 2
        for r, spread, one_hot in held(block) if keep else describe(block):
            near = [grid[pl.ds(start, win), (r * 2 + c) * q2 : (r * 2 + c + 1) * q2] for c in range(2)]
            values = dot(jnp.concatenate(near, 0).astype(BF), one_hot)
            for c in range(2):
                totals[c] = totals[c] + values[c * win : (c + 1) * win] * spread
        for c in range(2):
            out[block, c : c + 1] = jnp.sum(totals[c], 0, keepdims=True)
        return carry

    lax.fori_loop(0, blocks, collect, 0, unroll=UNROLL)


def recip_apply(meta, scale, rows_dev, *source):
    blocks, _, panels = meta.shape
    n1, n2 = scale.shape
    reach = n1 + window_rows(rows_dev)
    kept = [
        pltpu.VMEM((blocks, RADIX, n2 // RADIX, panels), BF),
        pltpu.VMEM((blocks, RADIX, window_rows(rows_dev), panels), F32),
    ]
    if held_bytes(meta.shape, rows_dev, n2) > MOST_HELD:
        kept = []
    tab1, tab2 = transform_tables(n1), transform_tables(n2)
    in_vmem = pl.BlockSpec(memory_space=pltpu.VMEM)
    return pl.pallas_call(
        functools.partial(recip_kernel, rows_dev, n1, n2),
        out_shape=jax.ShapeDtypeStruct((blocks, 2, panels), F32),
        in_specs=[in_vmem] * (4 + len(source)),
        out_specs=in_vmem,
        scratch_shapes=[
            pltpu.VMEM((reach, 2 * n2), F32),
            pltpu.VMEM((2 * RADIX, n1, n2 // RADIX), F32),
        ]
        + kept,
        compiler_params=pltpu.CompilerParams(vmem_limit_bytes=40 * 1024 * 1024),
        cost_estimate=pl.CostEstimate(
            flops=10_000_000_000, bytes_accessed=8_000_000, transcendentals=0
        ),
        name="recip",
    )(meta, scale, jnp.asarray(tab1), jnp.asarray(tab2), *source)


def border_phases(bloch):
    lane = lax.broadcasted_iota(jnp.int32, (1, 128), 1)
    angle = jnp.zeros((1, 128), F32)
    for k, (axis, offset) in enumerate(zip(AXES, (lane // 3 - 1, lane % 3 - 1))):
        place = lax.axis_index(axis) + offset
        leaves = (place < 0) | (place >= lax.axis_size(axis))
        angle += jnp.where(leaves, bloch[k] * offset.astype(F32), 0.0)
    return jnp.cos(angle), jnp.sin(angle)


def near_kernel(probes_first, bloch, halo, source, blocks, out):
    count, twice, _ = halo.shape
    probes = twice // 2
    cosines, sines = border_phases(bloch)
    total_real = 0.5 * source[0]
    total_imag = 0.5 * source[1]
    for d in range(count):
        x = halo[d]
        with_real = dot(x, blocks[0, d])
        with_imag = dot(x, blocks[1, d])
        real = with_real[:probes] - with_imag[probes:]
        imag = with_real[probes:] + with_imag[:probes]
        c = cosines[:, d : d + 1]
        s = sines[:, d : d + 1]
        total_real += real * c - imag * s
        total_imag += real * s + imag * c
    for c, total in enumerate((total_real, total_imag)):
        if probes_first:
            out[:, c, :] = total
        else:
            out[c] = total


def near_apply(halo, near_blocks, bloch_angle, source, probes_first):
    _, probes, panels = source.shape
    _, count, depth, _ = near_blocks.shape
    in_vmem = pl.BlockSpec(memory_space=pltpu.VMEM)
    shape = (probes, 2, panels) if probes_first else (2, probes, panels)
    return pl.pallas_call(
        functools.partial(near_kernel, probes_first),
        out_shape=jax.ShapeDtypeStruct(shape, F32),
        in_specs=[pl.BlockSpec(memory_space=pltpu.SMEM), in_vmem, in_vmem, in_vmem],
        out_specs=in_vmem,
        compiler_params=pltpu.CompilerParams(vmem_limit_bytes=8 * 1024 * 1024),
        cost_estimate=pl.CostEstimate(
            flops=4 * count * 2 * probes * depth * panels,
            bytes_accessed=2 * near_blocks.size,
            transcendentals=0,
        ),
        name="near",
    )(bloch_angle, halo, source, near_blocks)


def neighbour_kernel(tiles, sects, part, start, image, sent):
    image[...] = part[...] + start[...]

    def lay(block, carry):
        tile, sect = block // sects, block % sects
        rows = []
        for d in (-1, 0, 1):
            for e in (-1, 0, 1):
                near = (tile + d + tiles) % tiles * sects + (sect + e + sects) % sects
                rows.append(image[near])
        mine = image[block]
        hi = mine.astype(BF).astype(F32)
        mid = (mine - hi).astype(BF).astype(F32)
        rows += [mid, mine - hi - mid, jnp.zeros_like(mine)]
        sent[block] = jnp.concatenate(rows, 0).astype(BF)
        return carry

    lax.fori_loop(0, image.shape[0], lay, 0, unroll=4)


def neighbour_rows(part, start):
    blocks, _, panels = part.shape
    in_vmem = pl.BlockSpec(memory_space=pltpu.VMEM)
    return pl.pallas_call(
        functools.partial(neighbour_kernel, lax.axis_size("tile"), lax.axis_size("sect")),
        out_shape=(
            jax.ShapeDtypeStruct(part.shape, F32),
            jax.ShapeDtypeStruct((blocks, 24, panels), BF),
        ),
        in_specs=[in_vmem] * 2,
        out_specs=(in_vmem, in_vmem),
        compiler_params=pltpu.CompilerParams(vmem_limit_bytes=24 * 1024 * 1024),
        name="neighbour_rows",
    )(part, start)


def pack_kernel(rows_dev, groups, *refs):
    given, (sent, low), held, sems = refs[:4], refs[4:6], refs[6:10], refs[10]
    copies = [pltpu.make_async_copy(given[k], held[k], sems.at[k]) for k in range(4)]
    for copy in copies:
        copy.start()
    for copy in copies:
        copy.wait()
    source, stencil, first_row, first_col = held
    probes, panels = source.shape[1:]
    row, col = first_row[...], first_col[...]
    rest = col % RADIX
    given = [stencil[a].astype(F32) for a in range(STENCIL)]
    rows = []
    for a in range(STENCIL):
        for r in range(RADIX):
            taken = given[a][r : r + 1]
            for k in range(1, RADIX):
                b = (r - k) % RADIX
                taken = jnp.where(rest == k, given[a][b : b + 1], taken)
            rows.append(taken)
    rows.append((row % rows_dev).astype(F32))
    for r in range(RADIX):
        group = col // RADIX + jnp.where(rest > r, 1, 0)
        rows.append(jnp.where(group == groups, 0, group).astype(F32))
    rows.append(jnp.zeros((1, panels), F32))
    described = jnp.concatenate(rows, 0)
    for p in range(probes):
        value = [source[c, p : p + 1, :] for c in range(2)]
        sent[p] = jnp.concatenate(value + [described], 0).astype(BF)
    for c in range(2):
        low[c * probes : (c + 1) * probes] = source[c].astype(BF)


def pack(rows_dev, n2, source, stencil, grid_row, grid_col):
    _, probes, panels = source.shape
    rows = 2 + STENCIL * RADIX + 6
    in_vmem = pl.BlockSpec(memory_space=pltpu.VMEM)
    given = (source, stencil, grid_row[None], grid_col[None])
    return pl.pallas_call(
        functools.partial(pack_kernel, rows_dev, n2 // RADIX),
        out_shape=(
            jax.ShapeDtypeStruct((probes, rows, panels), BF),
            jax.ShapeDtypeStruct((2 * probes, panels), BF),
        ),
        in_specs=[pl.BlockSpec(memory_space=pl.ANY)] * 4,
        out_specs=(in_vmem, in_vmem),
        scratch_shapes=[pltpu.VMEM(x.shape, x.dtype) for x in given] + [pltpu.SemaphoreType.DMA((4,))],
        compiler_params=pltpu.CompilerParams(vmem_limit_bytes=60 * 1024 * 1024),
        name="pack",
    )(*given)


def shifted(array, axis, by):
    count = lax.axis_size(axis)
    return lax.ppermute(array, axis, [(i, (i + by) % count) for i in range(count)])


def beside(block, axis):
    return jnp.stack([shifted(block, axis, 1), block, shifted(block, axis, -1)])


def doubling_steps():
    return [(axis, 2**p) for axis in AXES[::-1] for p in range(11, -1, -1) if 2**p < lax.axis_size(axis)]


def doubled(block, step):
    axis, reach = step
    other = lax.ppermute(block, axis, [(i, i ^ reach) for i in range(lax.axis_size(axis))])
    upper = (lax.axis_index(axis) // reach) % 2 == 1
    return jnp.where(upper, jnp.stack([other, block]), jnp.stack([block, other]))


def in_columns(block, steps):
    held = steps[::-1]
    order = sorted(range(len(held)), key=lambda k: (AXES.index(held[k][0]), -held[k][1]))
    *_, columns, length = block.shape
    dims = len(held)
    whole = block.transpose([dims + 1] + order + [dims])
    return whole.reshape(length, columns * 2**dims)


def exchange(parts):
    return lax.all_to_all(parts, AXES, 0, 0, tiled=True)


def local(source_probes, near_blocks, bloch_angle, grid_row, grid_col, stencil, recip_kernel):
    count = lax.axis_size("tile") * lax.axis_size("sect")
    n1 = recip_kernel.shape[0]
    n2 = recip_kernel.shape[1] * count
    rows_dev = n1 // count
    _, probes, panels = source_probes.shape
    repeat = count // probes

    def to_owners(rows):
        return jnp.repeat(rows, repeat, axis=0) if repeat > 1 else rows

    def to_panels(rows):
        return exchange(rows)[::repeat]

    sent, low = pack(rows_dev, n2, source_probes, stencil, grid_row, grid_col)
    side = beside(low, "sect")
    steps = doubling_steps()
    kernel_rows = doubled(recip_kernel.astype(jnp.float16).T, steps[0])
    kernel_rows, side, sent = lax.optimization_barrier((kernel_rows, side, sent))
    meta = exchange(to_owners(sent))
    halo = beside(side, "tile").reshape(9, 2 * probes, panels)
    for step in steps[1:-1]:
        kernel_rows = doubled(kernel_rows, step)
    first_near = near_apply(halo, near_blocks, bloch_angle, source_probes, True)
    kernel_rows, first_near = lax.optimization_barrier((kernel_rows, first_near))
    scale = in_columns(doubled(kernel_rows, steps[-1]), steps).astype(F32) * (1.0 / (n1 * n2))
    start = exchange(to_owners(first_near))
    first_owned, spread = neighbour_rows(recip_apply(meta, scale, rows_dev), start)
    second_owned = recip_apply(meta, scale, rows_dev, first_owned)
    rows, second_owned = lax.optimization_barrier((to_panels(spread), second_owned))
    rows = rows.transpose(1, 0, 2)
    halo = rows[:18].reshape(9, 2 * probes, panels)
    first_image = rows[8:10].astype(F32) + rows[18:20].astype(F32) + rows[20:22].astype(F32)
    second_near = near_apply(halo, near_blocks, bloch_angle, first_image, False)
    second_image = second_near + to_panels(second_owned).transpose(1, 0, 2)
    return (first_image, second_image)


def solution(mesh):
    return jax.shard_map(
        local,
        mesh=mesh,
        in_specs=(
            P(None, "groups", AXES),
            P("groups", None, None, AXES),
            P("groups"),
            P(AXES),
            P(AXES),
            P(None, None, AXES),
            P("groups", AXES),
        ),
        out_specs=(P(None, "groups", AXES), P(None, "groups", AXES)),
        check_vma=False,
    )
```

```python
import functools

import jax
import jax.numpy as jnp
import ml_dtypes
import numpy as np
from jax import lax
from jax.experimental import pallas as pl
from jax.experimental.pallas import tpu as pltpu
from jax.sharding import PartitionSpec as P

STENCIL = 4
RADIX = 4
UNROLL = 16
MOST_HELD = 20 * 1024 * 1024
F32 = jnp.float32
BF = jnp.bfloat16
AXES = ("tile", "sect")


def split_host(x):
    hi = x.astype(ml_dtypes.bfloat16)
    lo = (x - hi.astype(np.float64)).astype(ml_dtypes.bfloat16)
    return np.stack([hi, lo])


def transform_tables(length):
    short = length // RADIX
    index = np.arange(short)
    tables = []
    for r in range(RADIX):
        angle = 2 * np.pi / length * (((RADIX * index[:, None] + r) * index[None, :]) % length)
        both = [np.cos(angle), np.sin(angle)]
        tables.append(
            np.stack([np.stack([split_host(x) for x in both]), np.stack([split_host(x.T) for x in both])])
        )
    return np.stack(tables)


def full_table(table, transposed):
    full = []
    for part in range(2):
        c, s = table[transposed, 0, part], table[transposed, 1, part]
        up, down = (s, -s) if transposed else (-s, s)
        full.append(jnp.concatenate([jnp.concatenate([c, up], 1), jnp.concatenate([down, c], 1)], 0))
    return full


def dot(a, b):
    return jnp.dot(a, b, preferred_element_type=F32)


def dot_last(a, b):
    return lax.dot_general(a, b, (((1,), (1,)), ((), ())), preferred_element_type=F32)


def split(x):
    hi = x.astype(BF)
    return hi, (x - hi.astype(F32)).astype(BF)


def times_right(x, table):
    hi, lo = split(x)
    rows = x.shape[0]
    y = dot(jnp.concatenate([hi, lo], 0), table[0])
    return y[:rows] + y[rows:] + dot(hi, table[1])


def times_left(table, x):
    hi, lo = split(x)
    rows = x.shape[0]
    y = dot(jnp.concatenate(table, 0), hi)
    return y[:rows] + y[rows:] + dot(table[0], lo)


def butterfly(parts, sign):
    (ar, ai), (br, bi), (cr, ci), (dr, di) = parts
    even_r, even_i, diff_r, diff_i = ar + cr, ai + ci, ar - cr, ai - ci
    odd_r, odd_i = br + dr, bi + di
    turn_r, turn_i = (di - bi, br - dr) if sign > 0 else (bi - di, dr - br)
    return [
        (even_r + odd_r, even_i + odd_i),
        (diff_r + turn_r, diff_i + turn_i),
        (even_r - odd_r, even_i - odd_i),
        (diff_r - turn_r, diff_i - turn_i),
    ]


def window_rows(rows_dev):
    lead = max((b * rows_dev) % 8 for b in range(8))
    return -(-(rows_dev + STENCIL - 1 + lead) // 8) * 8


def held_bytes(shape, rows_dev, n2):
    blocks, _, panels = shape
    return blocks * panels * RADIX * (2 * (n2 // RADIX) + 4 * window_rows(rows_dev))


def recip_kernel(rows_dev, n1, n2, meta, scale, tab1, tab2, *rest):
    keep = held_bytes(meta.shape, rows_dev, n2) <= MOST_HELD
    *source, out, grid, freq = rest[: len(rest) - 2 * keep]
    hot, weight = rest[len(rest) - 2 :]
    blocks, _, panels = meta.shape
    q1, q2 = n1 // RADIX, n2 // RADIX
    wide = 2 * q2
    win = window_rows(rows_dev)

    def start_of(block):
        return pl.multiple_of((block * rows_dev) // 8 * 8, 8)

    grid[...] = jnp.zeros_like(grid)

    def describe(block):
        rows = meta[block].astype(F32)
        offset = lax.broadcasted_iota(jnp.int32, (win, panels), 0).astype(F32)
        offset = offset - (rows[18:19] + (block * rows_dev - start_of(block)).astype(F32))
        at = [offset == float(a) for a in range(STENCIL)]
        lane = lax.broadcasted_iota(jnp.int32, (q2, panels), 0).astype(F32)
        for r in range(RADIX):
            spread = jnp.zeros((win, panels), F32)
            for a in range(STENCIL):
                k = 2 + a * RADIX + r
                spread = jnp.where(at[a], rows[k : k + 1], spread)
            one_hot = jnp.where(lane == rows[19 + r : 20 + r], 1.0, 0.0).astype(BF)
            yield r, spread, one_hot

    def scatter(block, carry):
        value = source[0][block].astype(BF).astype(F32) if source else meta[block].astype(F32)[0:2]
        start = start_of(block)
        for r, spread, one_hot in describe(block):
            if keep:
                weight[block, r] = spread
                hot[block, r] = one_hot
            both = jnp.concatenate([spread * value[c : c + 1] for c in range(2)], 0)
            sums = dot_last(jnp.concatenate(split(both), 0), one_hot)
            sums = sums[: 2 * win] + sums[2 * win :]
            for c in range(2):
                lanes = slice((r * 2 + c) * q2, (r * 2 + c + 1) * q2)
                grid[pl.ds(start, win), lanes] += sums[c * win : (c + 1) * win]
        return carry

    lax.fori_loop(0, blocks, scatter, 0, unroll=UNROLL)
    grid[0:win, :] += grid[n1 : n1 + win, :]

    parts = []
    for r in range(RADIX):
        y = times_right(grid[0:n1, r * wide : (r + 1) * wide], full_table(tab2.at[r], 0))
        parts.append((y[:, :q2], y[:, q2:]))
    for m, (real, imag) in enumerate(butterfly(parts, -1)):
        freq[2 * m] = real
        freq[2 * m + 1] = imag

    for pair in range(0, RADIX, 2):
        parts = []
        for r in range(RADIX):
            rows = pl.ds(r, q1, stride=RADIX)
            both = [
                jnp.concatenate([freq[2 * pair + c, rows, :], freq[2 * pair + 2 + c, rows, :]], 1)
                for c in range(2)
            ]
            y = times_left(full_table(tab1.at[r], 1), jnp.concatenate(both, 0))
            parts.append((y[:q1], y[q1:]))
        scaled = []
        for m, (real, imag) in enumerate(butterfly(parts, -1)):
            k = scale[m * q1 : (m + 1) * q1, pair * q2 : (pair + 2) * q2]
            scaled.append((real * k, imag * k))
        for r, both in enumerate(butterfly(scaled, 1)):
            y = times_left(full_table(tab1.at[r], 0), jnp.concatenate(both, 0))
            rows = pl.ds(r, q1, stride=RADIX)
            for c in range(2):
                freq[2 * pair + c, rows, :] = y[c * q1 : (c + 1) * q1, :q2]
                freq[2 * pair + 2 + c, rows, :] = y[c * q1 : (c + 1) * q1, q2:]

    parts = [(freq[2 * m], freq[2 * m + 1]) for m in range(RADIX)]
    for r, both in enumerate(butterfly(parts, 1)):
        grid[0:n1, r * wide : (r + 1) * wide] = times_right(jnp.concatenate(both, 1), full_table(tab2.at[r], 1))
    grid[n1 : n1 + win, :] = grid[0:win, :]

    def held(block):
        for r in range(RADIX):
            yield r, weight[block, r], hot[block, r]

    def collect(block, carry):
        start = start_of(block)
        totals = [jnp.zeros((win, panels), F32)] * 2
        for r, spread, one_hot in held(block) if keep else describe(block):
            near = [grid[pl.ds(start, win), (r * 2 + c) * q2 : (r * 2 + c + 1) * q2] for c in range(2)]
            values = dot(jnp.concatenate(near, 0).astype(BF), one_hot)
            for c in range(2):
                totals[c] = totals[c] + values[c * win : (c + 1) * win] * spread
        for c in range(2):
            out[block, c : c + 1] = jnp.sum(totals[c], 0, keepdims=True)
        return carry

    lax.fori_loop(0, blocks, collect, 0, unroll=UNROLL)


def recip_apply(meta, scale, rows_dev, *source):
    blocks, _, panels = meta.shape
    n1, n2 = scale.shape
    reach = n1 + window_rows(rows_dev)
    kept = [
        pltpu.VMEM((blocks, RADIX, n2 // RADIX, panels), BF),
        pltpu.VMEM((blocks, RADIX, window_rows(rows_dev), panels), F32),
    ]
    if held_bytes(meta.shape, rows_dev, n2) > MOST_HELD:
        kept = []
    tab1, tab2 = transform_tables(n1), transform_tables(n2)
    in_vmem = pl.BlockSpec(memory_space=pltpu.VMEM)
    return pl.pallas_call(
        functools.partial(recip_kernel, rows_dev, n1, n2),
        out_shape=jax.ShapeDtypeStruct((blocks, 2, panels), F32),
        in_specs=[in_vmem] * (4 + len(source)),
        out_specs=in_vmem,
        scratch_shapes=[
            pltpu.VMEM((reach, 2 * n2), F32),
            pltpu.VMEM((2 * RADIX, n1, n2 // RADIX), F32),
        ]
        + kept,
        compiler_params=pltpu.CompilerParams(vmem_limit_bytes=40 * 1024 * 1024),
        cost_estimate=pl.CostEstimate(
            flops=10_000_000_000, bytes_accessed=8_000_000, transcendentals=0
        ),
        name="recip",
    )(meta, scale, jnp.asarray(tab1), jnp.asarray(tab2), *source)


def border_phases(bloch):
    lane = lax.broadcasted_iota(jnp.int32, (1, 128), 1)
    angle = jnp.zeros((1, 128), F32)
    for k, (axis, offset) in enumerate(zip(AXES, (lane // 3 - 1, lane % 3 - 1))):
        place = lax.axis_index(axis) + offset
        leaves = (place < 0) | (place >= lax.axis_size(axis))
        angle += jnp.where(leaves, bloch[k] * offset.astype(F32), 0.0)
    return jnp.cos(angle), jnp.sin(angle)


def near_kernel(probes_first, bloch, halo, source, blocks, out):
    count, twice, _ = halo.shape
    probes = twice // 2
    cosines, sines = border_phases(bloch)
    total_real = 0.5 * source[0]
    total_imag = 0.5 * source[1]
    for d in range(count):
        x = halo[d]
        with_real = dot(x, blocks[0, d])
        with_imag = dot(x, blocks[1, d])
        real = with_real[:probes] - with_imag[probes:]
        imag = with_real[probes:] + with_imag[:probes]
        c = cosines[:, d : d + 1]
        s = sines[:, d : d + 1]
        total_real += real * c - imag * s
        total_imag += real * s + imag * c
    for c, total in enumerate((total_real, total_imag)):
        if probes_first:
            out[:, c, :] = total
        else:
            out[c] = total


def near_apply(halo, near_blocks, bloch_angle, source, probes_first):
    _, probes, panels = source.shape
    _, count, depth, _ = near_blocks.shape
    in_vmem = pl.BlockSpec(memory_space=pltpu.VMEM)
    shape = (probes, 2, panels) if probes_first else (2, probes, panels)
    return pl.pallas_call(
        functools.partial(near_kernel, probes_first),
        out_shape=jax.ShapeDtypeStruct(shape, F32),
        in_specs=[pl.BlockSpec(memory_space=pltpu.SMEM), in_vmem, in_vmem, in_vmem],
        out_specs=in_vmem,
        compiler_params=pltpu.CompilerParams(vmem_limit_bytes=8 * 1024 * 1024),
        cost_estimate=pl.CostEstimate(
            flops=4 * count * 2 * probes * depth * panels,
            bytes_accessed=2 * near_blocks.size,
            transcendentals=0,
        ),
        name="near",
    )(bloch_angle, halo, source, near_blocks)


def neighbour_kernel(tiles, sects, part, start, image, sent):
    image[...] = part[...] + start[...]

    def lay(block, carry):
        tile, sect = block // sects, block % sects
        rows = []
        for d in (-1, 0, 1):
            for e in (-1, 0, 1):
                near = (tile + d + tiles) % tiles * sects + (sect + e + sects) % sects
                rows.append(image[near])
        mine = image[block]
        hi = mine.astype(BF).astype(F32)
        mid = (mine - hi).astype(BF).astype(F32)
        rows += [mid, mine - hi - mid, jnp.zeros_like(mine)]
        sent[block] = jnp.concatenate(rows, 0).astype(BF)
        return carry

    lax.fori_loop(0, image.shape[0], lay, 0, unroll=4)


def neighbour_rows(part, start):
    blocks, _, panels = part.shape
    in_vmem = pl.BlockSpec(memory_space=pltpu.VMEM)
    return pl.pallas_call(
        functools.partial(neighbour_kernel, lax.axis_size("tile"), lax.axis_size("sect")),
        out_shape=(
            jax.ShapeDtypeStruct(part.shape, F32),
            jax.ShapeDtypeStruct((blocks, 24, panels), BF),
        ),
        in_specs=[in_vmem] * 2,
        out_specs=(in_vmem, in_vmem),
        compiler_params=pltpu.CompilerParams(vmem_limit_bytes=24 * 1024 * 1024),
        name="neighbour_rows",
    )(part, start)


def pack_kernel(rows_dev, groups, *refs):
    given, (sent, low), held, sems = refs[:4], refs[4:6], refs[6:10], refs[10]
    copies = [pltpu.make_async_copy(given[k], held[k], sems.at[k]) for k in range(4)]
    for copy in copies:
        copy.start()
    for copy in copies:
        copy.wait()
    source, stencil, first_row, first_col = held
    probes, panels = source.shape[1:]
    row, col = first_row[...], first_col[...]
    rest = col % RADIX
    given = [stencil[a].astype(F32) for a in range(STENCIL)]
    rows = []
    for a in range(STENCIL):
        for r in range(RADIX):
            taken = given[a][r : r + 1]
            for k in range(1, RADIX):
                b = (r - k) % RADIX
                taken = jnp.where(rest == k, given[a][b : b + 1], taken)
            rows.append(taken)
    rows.append((row % rows_dev).astype(F32))
    for r in range(RADIX):
        group = col // RADIX + jnp.where(rest > r, 1, 0)
        rows.append(jnp.where(group == groups, 0, group).astype(F32))
    rows.append(jnp.zeros((1, panels), F32))
    described = jnp.concatenate(rows, 0)
    for p in range(probes):
        value = [source[c, p : p + 1, :] for c in range(2)]
        sent[p] = jnp.concatenate(value + [described], 0).astype(BF)
    for c in range(2):
        low[c * probes : (c + 1) * probes] = source[c].astype(BF)


def pack(rows_dev, n2, source, stencil, grid_row, grid_col):
    _, probes, panels = source.shape
    rows = 2 + STENCIL * RADIX + 6
    in_vmem = pl.BlockSpec(memory_space=pltpu.VMEM)
    given = (source, stencil, grid_row[None], grid_col[None])
    return pl.pallas_call(
        functools.partial(pack_kernel, rows_dev, n2 // RADIX),
        out_shape=(
            jax.ShapeDtypeStruct((probes, rows, panels), BF),
            jax.ShapeDtypeStruct((2 * probes, panels), BF),
        ),
        in_specs=[pl.BlockSpec(memory_space=pl.ANY)] * 4,
        out_specs=(in_vmem, in_vmem),
        scratch_shapes=[pltpu.VMEM(x.shape, x.dtype) for x in given] + [pltpu.SemaphoreType.DMA((4,))],
        compiler_params=pltpu.CompilerParams(vmem_limit_bytes=60 * 1024 * 1024),
        name="pack",
    )(*given)


def shifted(array, axis, by):
    count = lax.axis_size(axis)
    return lax.ppermute(array, axis, [(i, (i + by) % count) for i in range(count)])


def beside(block, axis):
    return jnp.stack([shifted(block, axis, 1), block, shifted(block, axis, -1)])


def doubling_steps():
    return [(axis, 2**p) for axis in AXES[::-1] for p in range(11, -1, -1) if 2**p < lax.axis_size(axis)]


def doubled(block, step):
    axis, reach = step
    other = lax.ppermute(block, axis, [(i, i ^ reach) for i in range(lax.axis_size(axis))])
    upper = (lax.axis_index(axis) // reach) % 2 == 1
    return jnp.where(upper, jnp.stack([other, block]), jnp.stack([block, other]))


def in_columns(block, steps):
    held = steps[::-1]
    order = sorted(range(len(held)), key=lambda k: (AXES.index(held[k][0]), -held[k][1]))
    *_, columns, length = block.shape
    dims = len(held)
    whole = block.transpose([dims + 1] + order + [dims])
    return whole.reshape(length, columns * 2**dims)


def exchange(parts):
    return lax.all_to_all(parts, AXES, 0, 0, tiled=True)


def local(source_probes, near_blocks, bloch_angle, grid_row, grid_col, stencil, recip_kernel):
    count = lax.axis_size("tile") * lax.axis_size("sect")
    n1 = recip_kernel.shape[0]
    n2 = recip_kernel.shape[1] * count
    rows_dev = n1 // count
    _, probes, panels = source_probes.shape
    repeat = count // probes

    def to_owners(rows):
        return jnp.repeat(rows, repeat, axis=0) if repeat > 1 else rows

    def to_panels(rows):
        return exchange(rows)[::repeat]

    sent, low = pack(rows_dev, n2, source_probes, stencil, grid_row, grid_col)
    steps = doubling_steps()
    kernel_rows = doubled(recip_kernel.astype(jnp.float16).T, steps[0])
    kernel_rows, sent = lax.optimization_barrier((kernel_rows, sent))
    side = beside(low, "sect")
    meta = exchange(to_owners(sent))
    halo = beside(side, "tile").reshape(9, 2 * probes, panels)
    for step in steps[1:-1]:
        kernel_rows = doubled(kernel_rows, step)
    first_near = near_apply(halo, near_blocks, bloch_angle, source_probes, True)
    kernel_rows, first_near = lax.optimization_barrier((kernel_rows, first_near))
    scale = in_columns(doubled(kernel_rows, steps[-1]), steps).astype(F32) * (1.0 / (n1 * n2))
    start = exchange(to_owners(first_near))
    first_owned, spread = neighbour_rows(recip_apply(meta, scale, rows_dev), start)
    second_owned = recip_apply(meta, scale, rows_dev, first_owned)
    rows, second_owned = lax.optimization_barrier((to_panels(spread), second_owned))
    rows = rows.transpose(1, 0, 2)
    halo = rows[:18].reshape(9, 2 * probes, panels)
    first_image = rows[8:10].astype(F32) + rows[18:20].astype(F32) + rows[20:22].astype(F32)
    second_near = near_apply(halo, near_blocks, bloch_angle, first_image, False)
    second_image = second_near + to_panels(second_owned).transpose(1, 0, 2)
    return (first_image, second_image)


def solution(mesh):
    return jax.shard_map(
        local,
        mesh=mesh,
        in_specs=(
            P(None, "groups", AXES),
            P("groups", None, None, AXES),
            P("groups"),
            P(AXES),
            P(AXES),
            P(None, None, AXES),
            P("groups", AXES),
        ),
        out_specs=(P(None, "groups", AXES), P(None, "groups", AXES)),
        check_vma=False,
    )
```

```python
import functools

import jax
import jax.numpy as jnp
import ml_dtypes
import numpy as np
from jax import lax
from jax.experimental import pallas as pl
from jax.experimental.pallas import tpu as pltpu
from jax.sharding import PartitionSpec as P

STENCIL = 4
RADIX = 4
UNROLL = 16
GROUP = 4
MOST_HELD = 20 * 1024 * 1024
F32 = jnp.float32
BF = jnp.bfloat16
AXES = ("tile", "sect")


def split_host(x):
    hi = x.astype(ml_dtypes.bfloat16)
    lo = (x - hi.astype(np.float64)).astype(ml_dtypes.bfloat16)
    return np.stack([hi, lo])


def transform_tables(length):
    short = length // RADIX
    index = np.arange(short)
    tables = []
    for r in range(RADIX):
        angle = 2 * np.pi / length * (((RADIX * index[:, None] + r) * index[None, :]) % length)
        both = [np.cos(angle), np.sin(angle)]
        tables.append(
            np.stack([np.stack([split_host(x) for x in both]), np.stack([split_host(x.T) for x in both])])
        )
    return np.stack(tables)


def full_table(table, transposed):
    full = []
    for part in range(2):
        c, s = table[transposed, 0, part], table[transposed, 1, part]
        up, down = (s, -s) if transposed else (-s, s)
        full.append(jnp.concatenate([jnp.concatenate([c, up], 1), jnp.concatenate([down, c], 1)], 0))
    return full


def dot(a, b):
    return jnp.dot(a, b, preferred_element_type=F32)


def dot_last(a, b):
    return lax.dot_general(a, b, (((1,), (1,)), ((), ())), preferred_element_type=F32)


def split(x):
    hi = x.astype(BF)
    return hi, (x - hi.astype(F32)).astype(BF)


def times_right(x, table):
    hi, lo = split(x)
    rows = x.shape[0]
    y = dot(jnp.concatenate([hi, lo], 0), table[0])
    return y[:rows] + y[rows:] + dot(hi, table[1])


def times_left(table, x):
    hi, lo = split(x)
    rows = x.shape[0]
    y = dot(jnp.concatenate(table, 0), hi)
    return y[:rows] + y[rows:] + dot(table[0], lo)


def butterfly(parts, sign):
    (ar, ai), (br, bi), (cr, ci), (dr, di) = parts
    even_r, even_i, diff_r, diff_i = ar + cr, ai + ci, ar - cr, ai - ci
    odd_r, odd_i = br + dr, bi + di
    turn_r, turn_i = (di - bi, br - dr) if sign > 0 else (bi - di, dr - br)
    return [
        (even_r + odd_r, even_i + odd_i),
        (diff_r + turn_r, diff_i + turn_i),
        (even_r - odd_r, even_i - odd_i),
        (diff_r - turn_r, diff_i - turn_i),
    ]


def window_rows(rows_dev):
    lead = max((b * rows_dev) % 8 for b in range(8))
    return -(-(rows_dev + STENCIL - 1 + lead) // 8) * 8


def held_bytes(shape, rows_dev, n2):
    blocks, _, panels = shape
    return blocks * panels * RADIX * (2 * (n2 // RADIX) + 4 * window_rows(rows_dev))


def recip_kernel(rows_dev, n1, n2, meta, scale, tab1, tab2, *rest):
    keep = held_bytes(meta.shape, rows_dev, n2) <= MOST_HELD
    *source, out, grid, freq = rest[: len(rest) - 2 * keep]
    hot, weight = rest[len(rest) - 2 :]
    blocks, _, panels = meta.shape
    q1, q2 = n1 // RADIX, n2 // RADIX
    wide = 2 * q2
    win = window_rows(rows_dev)

    def start_of(block):
        return pl.multiple_of((block * rows_dev) // 8 * 8, 8)

    grid[...] = jnp.zeros_like(grid)

    def describe(block):
        rows = meta[block].astype(F32)
        offset = lax.broadcasted_iota(jnp.int32, (win, panels), 0).astype(F32)
        offset = offset - (rows[18:19] + (block * rows_dev - start_of(block)).astype(F32))
        at = [offset == float(a) for a in range(STENCIL)]
        lane = lax.broadcasted_iota(jnp.int32, (q2, panels), 0).astype(F32)
        for r in range(RADIX):
            spread = jnp.zeros((win, panels), F32)
            for a in range(STENCIL):
                k = 2 + a * RADIX + r
                spread = jnp.where(at[a], rows[k : k + 1], spread)
            one_hot = jnp.where(lane == rows[19 + r : 20 + r], 1.0, 0.0).astype(BF)
            yield r, spread, one_hot

    def scatter(block, carry):
        value = source[0][block].astype(BF).astype(F32) if source else meta[block].astype(F32)[0:2]
        start = start_of(block)
        for r, spread, one_hot in describe(block):
            if keep:
                weight[block, r] = spread
                hot[block, r] = one_hot
            both = jnp.concatenate([spread * value[c : c + 1] for c in range(2)], 0)
            sums = dot_last(jnp.concatenate(split(both), 0), one_hot)
            sums = sums[: 2 * win] + sums[2 * win :]
            for c in range(2):
                lanes = slice((r * 2 + c) * q2, (r * 2 + c + 1) * q2)
                grid[pl.ds(start, win), lanes] += sums[c * win : (c + 1) * win]
        return carry

    lax.fori_loop(0, blocks, scatter, 0, unroll=UNROLL)
    grid[0:win, :] += grid[n1 : n1 + win, :]

    parts = []
    for r in range(RADIX):
        y = times_right(grid[0:n1, r * wide : (r + 1) * wide], full_table(tab2.at[r], 0))
        parts.append((y[:, :q2], y[:, q2:]))
    for m, (real, imag) in enumerate(butterfly(parts, -1)):
        freq[2 * m] = real
        freq[2 * m + 1] = imag

    for first in range(0, RADIX, GROUP):
        group = range(first, first + GROUP)
        parts = []
        for r in range(RADIX):
            rows = pl.ds(r, q1, stride=RADIX)
            both = [jnp.concatenate([freq[2 * g + c, rows, :] for g in group], 1) for c in range(2)]
            y = times_left(full_table(tab1.at[r], 1), jnp.concatenate(both, 0))
            parts.append((y[:q1], y[q1:]))
        scaled = []
        for m, (real, imag) in enumerate(butterfly(parts, -1)):
            k = scale[m * q1 : (m + 1) * q1, first * q2 : (first + GROUP) * q2]
            scaled.append((real * k, imag * k))
        for r, both in enumerate(butterfly(scaled, 1)):
            y = times_left(full_table(tab1.at[r], 0), jnp.concatenate(both, 0))
            rows = pl.ds(r, q1, stride=RADIX)
            for k, g in enumerate(group):
                for c in range(2):
                    freq[2 * g + c, rows, :] = y[c * q1 : (c + 1) * q1, k * q2 : (k + 1) * q2]

    parts = [(freq[2 * m], freq[2 * m + 1]) for m in range(RADIX)]
    for r, both in enumerate(butterfly(parts, 1)):
        grid[0:n1, r * wide : (r + 1) * wide] = times_right(jnp.concatenate(both, 1), full_table(tab2.at[r], 1))
    grid[n1 : n1 + win, :] = grid[0:win, :]

    def held(block):
        for r in range(RADIX):
            yield r, weight[block, r], hot[block, r]

    def collect(block, carry):
        start = start_of(block)
        totals = [jnp.zeros((win, panels), F32)] * 2
        for r, spread, one_hot in held(block) if keep else describe(block):
            near = [grid[pl.ds(start, win), (r * 2 + c) * q2 : (r * 2 + c + 1) * q2] for c in range(2)]
            values = dot(jnp.concatenate(near, 0).astype(BF), one_hot)
            for c in range(2):
                totals[c] = totals[c] + values[c * win : (c + 1) * win] * spread
        for c in range(2):
            out[block, c : c + 1] = jnp.sum(totals[c], 0, keepdims=True)
        return carry

    lax.fori_loop(0, blocks, collect, 0, unroll=UNROLL)


def recip_apply(meta, scale, rows_dev, *source):
    blocks, _, panels = meta.shape
    n1, n2 = scale.shape
    reach = n1 + window_rows(rows_dev)
    kept = [
        pltpu.VMEM((blocks, RADIX, n2 // RADIX, panels), BF),
        pltpu.VMEM((blocks, RADIX, window_rows(rows_dev), panels), F32),
    ]
    if held_bytes(meta.shape, rows_dev, n2) > MOST_HELD:
        kept = []
    tab1, tab2 = transform_tables(n1), transform_tables(n2)
    in_vmem = pl.BlockSpec(memory_space=pltpu.VMEM)
    return pl.pallas_call(
        functools.partial(recip_kernel, rows_dev, n1, n2),
        out_shape=jax.ShapeDtypeStruct((blocks, 2, panels), F32),
        in_specs=[in_vmem] * (4 + len(source)),
        out_specs=in_vmem,
        scratch_shapes=[
            pltpu.VMEM((reach, 2 * n2), F32),
            pltpu.VMEM((2 * RADIX, n1, n2 // RADIX), F32),
        ]
        + kept,
        compiler_params=pltpu.CompilerParams(vmem_limit_bytes=40 * 1024 * 1024),
        cost_estimate=pl.CostEstimate(
            flops=10_000_000_000, bytes_accessed=8_000_000, transcendentals=0
        ),
        name="recip",
    )(meta, scale, jnp.asarray(tab1), jnp.asarray(tab2), *source)


def border_phases(bloch):
    lane = lax.broadcasted_iota(jnp.int32, (1, 128), 1)
    angle = jnp.zeros((1, 128), F32)
    for k, (axis, offset) in enumerate(zip(AXES, (lane // 3 - 1, lane % 3 - 1))):
        place = lax.axis_index(axis) + offset
        leaves = (place < 0) | (place >= lax.axis_size(axis))
        angle += jnp.where(leaves, bloch[k] * offset.astype(F32), 0.0)
    return jnp.cos(angle), jnp.sin(angle)


def near_kernel(probes_first, bloch, halo, source, blocks, out):
    count, twice, _ = halo.shape
    probes = twice // 2
    cosines, sines = border_phases(bloch)
    total_real = 0.5 * source[0]
    total_imag = 0.5 * source[1]
    for d in range(count):
        x = halo[d]
        with_real = dot(x, blocks[0, d])
        with_imag = dot(x, blocks[1, d])
        real = with_real[:probes] - with_imag[probes:]
        imag = with_real[probes:] + with_imag[:probes]
        c = cosines[:, d : d + 1]
        s = sines[:, d : d + 1]
        total_real += real * c - imag * s
        total_imag += real * s + imag * c
    for c, total in enumerate((total_real, total_imag)):
        if probes_first:
            out[:, c, :] = total
        else:
            out[c] = total


def near_apply(halo, near_blocks, bloch_angle, source, probes_first):
    _, probes, panels = source.shape
    _, count, depth, _ = near_blocks.shape
    in_vmem = pl.BlockSpec(memory_space=pltpu.VMEM)
    shape = (probes, 2, panels) if probes_first else (2, probes, panels)
    return pl.pallas_call(
        functools.partial(near_kernel, probes_first),
        out_shape=jax.ShapeDtypeStruct(shape, F32),
        in_specs=[pl.BlockSpec(memory_space=pltpu.SMEM), in_vmem, in_vmem, in_vmem],
        out_specs=in_vmem,
        compiler_params=pltpu.CompilerParams(vmem_limit_bytes=8 * 1024 * 1024),
        cost_estimate=pl.CostEstimate(
            flops=4 * count * 2 * probes * depth * panels,
            bytes_accessed=2 * near_blocks.size,
            transcendentals=0,
        ),
        name="near",
    )(bloch_angle, halo, source, near_blocks)


def neighbour_kernel(tiles, sects, part, start, image, sent):
    image[...] = part[...] + start[...]

    def lay(block, carry):
        tile, sect = block // sects, block % sects
        rows = []
        for d in (-1, 0, 1):
            for e in (-1, 0, 1):
                near = (tile + d + tiles) % tiles * sects + (sect + e + sects) % sects
                rows.append(image[near])
        mine = image[block]
        hi = mine.astype(BF).astype(F32)
        mid = (mine - hi).astype(BF).astype(F32)
        rows += [mid, mine - hi - mid, jnp.zeros_like(mine)]
        sent[block] = jnp.concatenate(rows, 0).astype(BF)
        return carry

    lax.fori_loop(0, image.shape[0], lay, 0, unroll=4)


def neighbour_rows(part, start):
    blocks, _, panels = part.shape
    in_vmem = pl.BlockSpec(memory_space=pltpu.VMEM)
    return pl.pallas_call(
        functools.partial(neighbour_kernel, lax.axis_size("tile"), lax.axis_size("sect")),
        out_shape=(
            jax.ShapeDtypeStruct(part.shape, F32),
            jax.ShapeDtypeStruct((blocks, 24, panels), BF),
        ),
        in_specs=[in_vmem] * 2,
        out_specs=(in_vmem, in_vmem),
        compiler_params=pltpu.CompilerParams(vmem_limit_bytes=24 * 1024 * 1024),
        name="neighbour_rows",
    )(part, start)


def pack_kernel(rows_dev, groups, *refs):
    given, (sent, low), held, sems = refs[:4], refs[4:6], refs[6:10], refs[10]
    copies = [pltpu.make_async_copy(given[k], held[k], sems.at[k]) for k in range(4)]
    for copy in copies:
        copy.start()
    for copy in copies:
        copy.wait()
    source, stencil, first_row, first_col = held
    probes, panels = source.shape[1:]
    row, col = first_row[...], first_col[...]
    rest = col % RADIX
    given = [stencil[a].astype(F32) for a in range(STENCIL)]
    rows = []
    for a in range(STENCIL):
        for r in range(RADIX):
            taken = given[a][r : r + 1]
            for k in range(1, RADIX):
                b = (r - k) % RADIX
                taken = jnp.where(rest == k, given[a][b : b + 1], taken)
            rows.append(taken)
    rows.append((row % rows_dev).astype(F32))
    for r in range(RADIX):
        group = col // RADIX + jnp.where(rest > r, 1, 0)
        rows.append(jnp.where(group == groups, 0, group).astype(F32))
    rows.append(jnp.zeros((1, panels), F32))
    described = jnp.concatenate(rows, 0)
    for p in range(probes):
        value = [source[c, p : p + 1, :] for c in range(2)]
        sent[p] = jnp.concatenate(value + [described], 0).astype(BF)
    for c in range(2):
        low[c * probes : (c + 1) * probes] = source[c].astype(BF)


def pack(rows_dev, n2, source, stencil, grid_row, grid_col):
    _, probes, panels = source.shape
    rows = 2 + STENCIL * RADIX + 6
    in_vmem = pl.BlockSpec(memory_space=pltpu.VMEM)
    given = (source, stencil, grid_row[None], grid_col[None])
    return pl.pallas_call(
        functools.partial(pack_kernel, rows_dev, n2 // RADIX),
        out_shape=(
            jax.ShapeDtypeStruct((probes, rows, panels), BF),
            jax.ShapeDtypeStruct((2 * probes, panels), BF),
        ),
        in_specs=[pl.BlockSpec(memory_space=pl.ANY)] * 4,
        out_specs=(in_vmem, in_vmem),
        scratch_shapes=[pltpu.VMEM(x.shape, x.dtype) for x in given] + [pltpu.SemaphoreType.DMA((4,))],
        compiler_params=pltpu.CompilerParams(vmem_limit_bytes=60 * 1024 * 1024),
        name="pack",
    )(*given)


def shifted(array, axis, by):
    count = lax.axis_size(axis)
    return lax.ppermute(array, axis, [(i, (i + by) % count) for i in range(count)])


def beside(block, axis):
    return jnp.stack([shifted(block, axis, 1), block, shifted(block, axis, -1)])


def doubling_steps():
    return [(axis, 2**p) for axis in AXES[::-1] for p in range(11, -1, -1) if 2**p < lax.axis_size(axis)]


def doubled(block, step):
    axis, reach = step
    other = lax.ppermute(block, axis, [(i, i ^ reach) for i in range(lax.axis_size(axis))])
    upper = (lax.axis_index(axis) // reach) % 2 == 1
    return jnp.where(upper, jnp.stack([other, block]), jnp.stack([block, other]))


def in_columns(block, steps):
    held = steps[::-1]
    order = sorted(range(len(held)), key=lambda k: (AXES.index(held[k][0]), -held[k][1]))
    *_, columns, length = block.shape
    dims = len(held)
    whole = block.transpose([dims + 1] + order + [dims])
    return whole.reshape(length, columns * 2**dims)


def exchange(parts):
    return lax.all_to_all(parts, AXES, 0, 0, tiled=True)


def local(source_probes, near_blocks, bloch_angle, grid_row, grid_col, stencil, recip_kernel):
    count = lax.axis_size("tile") * lax.axis_size("sect")
    n1 = recip_kernel.shape[0]
    n2 = recip_kernel.shape[1] * count
    rows_dev = n1 // count
    _, probes, panels = source_probes.shape
    repeat = count // probes

    def to_owners(rows):
        return jnp.repeat(rows, repeat, axis=0) if repeat > 1 else rows

    def to_panels(rows):
        return exchange(rows)[::repeat]

    sent, low = pack(rows_dev, n2, source_probes, stencil, grid_row, grid_col)
    steps = doubling_steps()
    kernel_rows = doubled(recip_kernel.astype(jnp.float16).T, steps[0])
    kernel_rows, sent = lax.optimization_barrier((kernel_rows, sent))
    side = beside(low, "sect")
    meta = exchange(to_owners(sent))
    halo = beside(side, "tile").reshape(9, 2 * probes, panels)
    for step in steps[1:-1]:
        kernel_rows = doubled(kernel_rows, step)
    first_near = near_apply(halo, near_blocks, bloch_angle, source_probes, True)
    kernel_rows, first_near = lax.optimization_barrier((kernel_rows, first_near))
    scale = in_columns(doubled(kernel_rows, steps[-1]), steps).astype(F32) * (1.0 / (n1 * n2))
    start = exchange(to_owners(first_near))
    first_owned, spread = neighbour_rows(recip_apply(meta, scale, rows_dev), start)
    second_owned = recip_apply(meta, scale, rows_dev, first_owned)
    rows, second_owned = lax.optimization_barrier((to_panels(spread), second_owned))
    rows = rows.transpose(1, 0, 2)
    halo = rows[:18].reshape(9, 2 * probes, panels)
    first_image = rows[8:10].astype(F32) + rows[18:20].astype(F32) + rows[20:22].astype(F32)
    second_near = near_apply(halo, near_blocks, bloch_angle, first_image, False)
    second_image = second_near + to_panels(second_owned).transpose(1, 0, 2)
    return (first_image, second_image)


def solution(mesh):
    return jax.shard_map(
        local,
        mesh=mesh,
        in_specs=(
            P(None, "groups", AXES),
            P("groups", None, None, AXES),
            P("groups"),
            P(AXES),
            P(AXES),
            P(None, None, AXES),
            P("groups", AXES),
        ),
        out_specs=(P(None, "groups", AXES), P(None, "groups", AXES)),
        check_vma=False,
    )
```
